256 devices in a mesh: outer: 16 (over z, y_hi), local: 8 (over x, core), split: 2 (over y_lo).
Axes of the slice: x: 4, y: 4 (y_hi: 2, y_lo: 2; y = y_hi * 2 + y_lo), z: 8, core: 2. Of those that a mesh axis runs over, the one named last changes fastest.
Arguments:
- tokens: bfloat16 [16384, 2048], P(('outer', 'local')), may hold values from -11 to 11
- grad_out: bfloat16 [16384, 2048], P(('outer', 'local')), may hold values from -1.5 to 1.5
- router_weight: bfloat16 [2048, 128], replicated, may hold values from -0.11269514 to 0.11269514
- expert_ids: int32 [16384, 8], P(('outer', 'local')), may hold values from 0 to 127, as said below
- gate_fixed: int32 [16384, 8], P(('outer', 'local')), may hold values from 1 to 65535
- w_gate: bfloat16 [128, 2048, 768], P(('outer', 'local'), None, 'split'), may hold values from -0.125 to 0.125
- w_up: bfloat16 [128, 2048, 768], P(('outer', 'local'), None, 'split'), may hold values from -0.125 to 0.125
- w_down: bfloat16 [128, 768, 2048], P(('outer', 'local'), 'split'), may hold values from -0.21875 to 0.21875
Outputs:
- grad_tokens: bfloat16 [16384, 2048], P(('outer', 'local', 'split'))
- d_gate: float32 [16384, 8], P(('outer', 'local', 'split'))
- d_logits: float32 [16384, 128], P(('outer', 'local', 'split'))
The draws below stay inside these ranges and needn't reach their ends.
Inputs may be any that keep to these rules, and one draw needn't show every extreme that they name: `expert_ids`: each row names 8 different experts. The 128 rows of one index of outer and local name one expert at most 12 times, and some expert exactly 12 times; over all rows one expert is named at most 1280 times, and some expert exactly 1280 times.
All inputs are finite; a program needn't handle non-finite values.
Results may differ from the reference program's by a relative error of at most 0.022.
Values may be sent and summed in bfloat16 or wider, within the bound.
No kernel may reach another device: no remote copies, remote signals or barrier semaphores. Data moves between devices by JAX's collectives and lax.ppermute only.
A program may use at most 128 MiB of HBM per device.

```python
import jax
import jax.numpy as jnp
from jax import lax

D = 2048
FF = 768
TOPK = 8
TOK_DEV = 128
EXPERTS = 128
FF_DEV = 384
TOKENS = 16384
RMAX = 1280
N_SPLIT = 2


def router_matrix(key):
    first_key = jax.random.fold_in(key, 0)
    normal_part = jnp.clip(jax.random.normal(first_key, (D, EXPERTS), jnp.float32), -5.0, 5.0)
    return normal_part * D ** (-0.5)


def draw_router_weight(key, part):
    return router_matrix(key).astype(jnp.bfloat16)


def draw_tokens(key, part):
    key = jax.random.fold_in(key, 21)
    keys = jax.random.split(key, 7)
    values = jnp.clip(jax.random.normal(keys[6], (TOKENS, D), jnp.float32), -5.0, 5.0)
    return values.astype(jnp.bfloat16)


def draw_expert_ids(key, part):
    key = jax.random.fold_in(key, 7)
    first_key, second_key, third_key = jax.random.split(key, 3)
    quarter = TOK_DEV * TOPK // (4 * EXPERTS)
    position = jnp.arange(EXPERTS, dtype=jnp.int32)
    level = jnp.where(position < EXPERTS // 4, 6 * quarter, jnp.where(position < EXPERTS // 2, 4 * quarter, 3 * quarter))
    offset = jax.random.randint(first_key, (), 0, EXPERTS)
    source = jnp.arange(EXPERTS, dtype=jnp.int32)
    shifted = offset + source // 2
    counts = level[(position[None, :] - shifted[:, None]) % EXPERTS]
    ends = jnp.cumsum(counts, axis=1)
    entry = jnp.arange(TOK_DEV * TOPK, dtype=jnp.int32)
    owner = jnp.sum((ends[:, None, :] <= entry[None, :, None]).astype(jnp.int32), axis=2)
    table = owner.reshape(EXPERTS, TOPK, TOK_DEV).transpose(0, 2, 1)
    row_keys = jax.random.split(second_key, EXPERTS)
    row_order = jax.vmap(lambda one_key: jax.random.permutation(one_key, TOK_DEV))(row_keys)
    table = jnp.take_along_axis(table, row_order[:, :, None], axis=1)
    scores = jax.random.randint(third_key, (EXPERTS, TOK_DEV, TOPK), 0, 1 << 20) * TOPK + jnp.arange(TOPK, dtype=jnp.int32)
    columns = jnp.argsort(scores, axis=2)
    table = jnp.take_along_axis(table, columns, axis=2)
    return table.reshape(TOKENS, TOPK).astype(jnp.int32)


def with_ends(values, own_key, least, high):
    longest = values.shape.index(max(values.shape))
    spots = []
    for shift in (0, 1):
        where = [jax.random.randint(jax.random.fold_in(own_key, axis), (), 0, length) for axis, length in enumerate(values.shape)]
        where[longest] = (where[longest] + shift) % values.shape[longest]
        spots.append(tuple(where))
    return values.at[spots[0]].set(least).at[spots[1]].set(high)


def block_scale(stream_key, shape, pieces, smallest, high):
    loudness, own = 1.0, jax.random.fold_in(stream_key, 6)
    for axis_at, parts in pieces:
        steps = jnp.exp(jax.random.uniform(jax.random.fold_in(own, axis_at), (parts,), jnp.float32, smallest / len(pieces), high / len(pieces)))
        loudness = loudness * jnp.repeat(steps, shape[axis_at] // parts).reshape([-1 if axis == axis_at else 1 for axis in range(len(shape))])
    return loudness


def centred(key, extent, deviation, limit, pieces=(), kind=jnp.bfloat16):
    level = block_scale(key, extent, pieces, -0.22, 0.18) if pieces else 1.0
    values = jax.random.normal(key, extent, jnp.float32) * deviation * level
    return jnp.minimum(jnp.maximum(values, -limit), limit).astype(kind)


def setup_inputs(seed: int = 0) -> dict:
    streams_of = jax.random.split(jax.random.key(seed), 9)
    return {
        "tokens": draw_tokens(jax.random.fold_in(streams_of[8], 71), 0),
        "grad_out": centred(streams_of[1], (TOKENS, D), 0.25, 1.5, ((0, 128),)),
        "router_weight": draw_router_weight(jax.random.fold_in(streams_of[8], 71), 0),
        "expert_ids": draw_expert_ids(jax.random.fold_in(streams_of[8], 71), 0),
        "gate_fixed": with_ends(jax.random.randint(streams_of[4], (TOKENS, TOPK), 1, 65536), jax.random.fold_in(streams_of[4], 1), 1, 65535).astype(jnp.int32),
        "w_gate": centred(streams_of[5], (EXPERTS, D, FF), D ** -0.5, 0.125, ((0, 128), (2, 2))),
        "w_up": centred(streams_of[6], (EXPERTS, D, FF), D ** -0.5, 0.125, ((0, 128), (2, 2))),
        "w_down": centred(streams_of[7], (EXPERTS, FF, D), FF ** -0.5, 0.21875, ((0, 128), (1, 2))),
    }


def expert_block(flat_x, flat_dy, gate_vals, block_gate, block_up, block_down):
    contract = (((1,), (1,)), ((), ()))
    pre_gate = jnp.dot(flat_x, block_gate, preferred_element_type=jnp.float32)
    pre_up = jnp.dot(flat_x, block_up, preferred_element_type=jnp.float32)
    sigmoid_gate = jax.nn.sigmoid(pre_gate)
    activated = pre_gate * sigmoid_gate
    hidden = (activated * pre_up).astype(jnp.bfloat16)
    output = jnp.dot(hidden, block_down, preferred_element_type=jnp.float32)
    gate_term = jnp.sum(flat_dy.astype(jnp.float32) * output, axis=1).astype(jnp.bfloat16)
    scaled = (gate_vals[:, None] * flat_dy.astype(jnp.float32)).astype(jnp.bfloat16)
    d_hidden = lax.dot_general(scaled, block_down, contract, preferred_element_type=jnp.float32)
    d_pre_gate = (d_hidden * pre_up * sigmoid_gate * (1.0 + pre_gate * (1.0 - sigmoid_gate))).astype(jnp.bfloat16)
    d_pre_up = (d_hidden * activated).astype(jnp.bfloat16)
    row_grad = lax.dot_general(d_pre_gate, block_gate, contract, preferred_element_type=jnp.float32)
    row_grad = row_grad + lax.dot_general(d_pre_up, block_up, contract, preferred_element_type=jnp.float32)
    return row_grad.astype(jnp.bfloat16), gate_term


def reference(tokens, grad_out, router_weight, expert_ids, gate_fixed, w_gate, w_up, w_down):
    flat_ids = expert_ids.reshape(-1).astype(jnp.int32)
    order = jnp.argsort(flat_ids, stable=True).astype(jnp.int32)
    load = jnp.sum((flat_ids[:, None] == jnp.arange(EXPERTS, dtype=jnp.int32)[None, :]).astype(jnp.int32), axis=0)
    starts = (jnp.cumsum(load) - load).astype(jnp.int32)
    padded = jnp.concatenate([order, jnp.zeros((RMAX,), jnp.int32)])
    gate = gate_fixed.reshape(-1).astype(jnp.float32) / 65536.0

    def per_expert(carry, item):
        grad_acc, gate_acc = carry
        expert, own_gate, own_up, own_down = item
        entries = lax.dynamic_slice(padded, (starts[expert].astype(jnp.int32),), (RMAX,))
        live = jnp.arange(RMAX, dtype=jnp.int32) < load[expert]
        rows = (entries // TOPK).astype(jnp.int32)
        flat_x = tokens[rows]
        flat_dy = grad_out[rows]
        gate_vals = gate[entries]
        grad_rows = jnp.zeros((RMAX, D), jnp.float32)
        gate_rows = jnp.zeros((RMAX,), jnp.float32)
        for block in range(N_SPLIT):
            first = block * FF_DEV
            block_grad, block_term = expert_block(flat_x, flat_dy, gate_vals, own_gate[:, first:first + FF_DEV], own_up[:, first:first + FF_DEV], own_down[first:first + FF_DEV, :])
            grad_rows = grad_rows + block_grad.astype(jnp.float32)
            gate_rows = gate_rows + block_term.astype(jnp.float32)
        pair_grad = lax.optimization_barrier(grad_rows.astype(jnp.bfloat16))
        grad_rows = pair_grad.astype(jnp.float32)
        grad_rows = jnp.where(live[:, None], grad_rows, jnp.zeros_like(grad_rows))
        gate_rows = jnp.where(live, gate_rows, jnp.zeros_like(gate_rows))
        grad_acc = grad_acc.at[rows].add(grad_rows)
        gate_acc = gate_acc.at[entries].add(gate_rows)
        return (grad_acc, gate_acc), None

    start_carry = (jnp.zeros((TOKENS, D), jnp.float32), jnp.zeros((TOKENS * TOPK,), jnp.float32))
    (expert_grad, gate_flat), _ = lax.scan(per_expert, start_carry, (jnp.arange(EXPERTS, dtype=jnp.int32), w_gate, w_up, w_down))
    d_gate = gate_flat.reshape(TOKENS, TOPK)
    logits = jnp.dot(tokens, router_weight, preferred_element_type=jnp.float32)
    probs = jax.nn.softmax(logits, axis=1)
    share = load.astype(jnp.float32) * EXPERTS / (TOKENS * TOPK)
    d_logits = EXPERTS * probs * (share[None, :] - jnp.sum(probs * share[None, :], axis=1, keepdims=True))
    contract = (((1,), (1,)), ((), ()))
    router_back = lax.dot_general(d_logits.astype(jnp.bfloat16), router_weight, contract, preferred_element_type=jnp.float32)
    grad_tokens = (expert_grad + router_back).astype(jnp.bfloat16)
    return grad_tokens, d_gate, d_logits
```

```python
import jax
import jax.numpy as jnp
import numpy as np
from jax import lax
from jax.experimental import pallas as pl
from jax.experimental.pallas import tpu as pltpu
from jax.sharding import Mesh
from jax.sharding import PartitionSpec as P

EXPERTS = 128
Z = 8
PLANE_EXPERTS = 16
TOK = 128
COL = Z * TOK
WIDTH = 2048
HALF = 1024
META = 128
SLOTS = 48
GROUPS = 32
ROWS = GROUPS * SLOTS
RECV = 16 * SLOTS
FF = 384
TOPK = 8
F32 = jnp.float32
BF16 = jnp.bfloat16
PLANE = ("yh", "x", "c", "yl")


def group_expert(g):
    return (g // 4) * 2 + g % 2


def group_first(g):
    return ((g // 2) % 2) * SLOTS


def slot_tables():
    group = np.arange(ROWS) // SLOTS
    expert = (group // 4) * 2 + group % 2
    rank = ((group // 2) % 2) * SLOTS + np.arange(ROWS) % SLOTS
    pick_rank = (np.arange(128)[:, None] == expert[None, :]).astype(np.float32)
    pick_gate = (np.arange(128)[:, None] == expert[None, :] + PLANE_EXPERTS).astype(np.float32)
    rank_row = np.broadcast_to(rank[None, :], (8, ROWS)).astype(np.float32)
    return jnp.asarray(pick_rank, BF16), jnp.asarray(pick_gate, BF16), jnp.asarray(rank_row, F32)


def route_kernel(plane_ref, meta_ref, rank_ref, turned_ref, count_ref, rank_all, gate_all):
    turned = meta_ref[...].astype(F32).T
    expert = lax.broadcasted_iota(jnp.int32, (EXPERTS, COL), 0).astype(F32)
    member = jnp.zeros((EXPERTS, COL), F32)
    gate = jnp.zeros((EXPERTS, COL), F32)
    for k in range(TOPK):
        same = turned[k : k + 1, :] == expert
        value = (turned[8 + k : 9 + k, :] * 256.0 + turned[16 + k : 17 + k, :]) * (1.0 / 65536.0)
        member = member + jnp.where(same, 1.0, 0.0)
        gate = gate + jnp.where(same, value, 0.0)
    row = lax.broadcasted_iota(jnp.int32, (COL, COL), 0)
    column = lax.broadcasted_iota(jnp.int32, (COL, COL), 1)
    before = jnp.where(row < column, 1.0, 0.0).astype(BF16)
    low = member.astype(BF16)
    rank = jnp.dot(low, before, preferred_element_type=F32)
    rank_all[...] = jnp.where(member > 0.0, rank, -1.0)
    gate_all[...] = gate
    first = pl.multiple_of(plane_ref[0] * PLANE_EXPERTS, PLANE_EXPERTS)
    rank16 = rank_all[pl.ds(first, PLANE_EXPERTS), :]
    gate16 = gate_all[pl.ds(first, PLANE_EXPERTS), :]
    rank_ref[...] = rank16
    rest = jnp.zeros((128 - 2 * PLANE_EXPERTS, COL), F32)
    turned_ref[...] = jnp.concatenate([rank16, gate16, rest], axis=0).T
    count_ref[...] = lax.dot_general(
        jnp.ones((8, COL), BF16), low, (((1,), (1,)), ((), ())), preferred_element_type=F32
    )


def route(plane, gathered):
    return pl.pallas_call(
        route_kernel,
        grid_spec=pltpu.PrefetchScalarGridSpec(
            num_scalar_prefetch=1,
            grid=(1,),
            in_specs=[pl.BlockSpec((COL, META), lambda i, s: (0, HALF // META))],
            out_specs=[
                pl.BlockSpec((PLANE_EXPERTS, COL), lambda i, s: (0, 0)),
                pl.BlockSpec((COL, 128), lambda i, s: (0, 0)),
                pl.BlockSpec((8, EXPERTS), lambda i, s: (0, 0)),
            ],
            scratch_shapes=[pltpu.VMEM((EXPERTS, COL), F32), pltpu.VMEM((EXPERTS, COL), F32)],
        ),
        out_shape=[
            jax.ShapeDtypeStruct((PLANE_EXPERTS, COL), F32),
            jax.ShapeDtypeStruct((COL, 128), F32),
            jax.ShapeDtypeStruct((8, EXPERTS), F32),
        ],
        compiler_params=pltpu.CompilerParams(vmem_limit_bytes=24 << 20),
        cost_estimate=pl.CostEstimate(flops=300000000, bytes_accessed=1000000, transcendentals=0),
        name="route",
    )(plane, gathered)


def dispatch_kernel(rank_ref, rows_ref, out_ref, place):
    @pl.when(pl.program_id(0) == 0)
    def _():
        slot = lax.broadcasted_iota(jnp.int32, (SLOTS, COL), 0).astype(F32)
        for g in range(GROUPS):
            e = group_expert(g)
            hit = slot + float(group_first(g)) == rank_ref[e : e + 1, :]
            place[g * SLOTS : (g + 1) * SLOTS, :] = jnp.where(hit, 1.0, 0.0).astype(BF16)

    part = jnp.dot(place[...], rows_ref[...], preferred_element_type=F32)
    out_ref[...] = part.astype(BF16).reshape(out_ref.shape)


def dispatch(rank, rows):
    block = 256
    return pl.pallas_call(
        dispatch_kernel,
        grid=(HALF // block,),
        in_specs=[
            pl.BlockSpec((PLANE_EXPERTS, COL), lambda i: (0, 0)),
            pl.BlockSpec((COL, block), lambda i: (0, i)),
        ],
        out_specs=pl.BlockSpec((GROUPS, SLOTS, block), lambda i: (0, 0, i)),
        out_shape=jax.ShapeDtypeStruct((GROUPS, SLOTS, HALF), BF16),
        scratch_shapes=[pltpu.VMEM((ROWS, COL), BF16)],
        compiler_params=pltpu.CompilerParams(vmem_limit_bytes=24 << 20),
        cost_estimate=pl.CostEstimate(flops=2 * ROWS * COL * HALF, bytes_accessed=5500000, transcendentals=0),
        name="dispatch",
    )(rank, rows)


def forward_kernel(x_ref, gate_a, gate_b, up_a, up_b, pre_gate_ref, pre_up_ref):
    low = x_ref[:, 0].reshape(-1, HALF)
    high = x_ref[:, 1].reshape(-1, HALF)
    for i, (gate, up) in enumerate(((gate_a, up_a), (gate_b, up_b))):
        for weight, out in ((gate, pre_gate_ref), (up, pre_up_ref)):
            out[:, i * FF : (i + 1) * FF] = jnp.dot(
                low, weight[:HALF, :], preferred_element_type=F32
            ) + jnp.dot(high, weight[HALF:, :], preferred_element_type=F32)


def forward(x_recv, gate_a, gate_b, up_a, up_b):
    steps = 4
    weight = pl.BlockSpec((WIDTH, FF), lambda i: (0, 0))
    out = pl.BlockSpec((RECV // steps, 2 * FF), lambda i: (i, 0))
    return pl.pallas_call(
        forward_kernel,
        grid=(steps,),
        in_specs=[pl.BlockSpec((16 // steps, 2, SLOTS, HALF), lambda i: (i, 0, 0, 0))] + [weight] * 4,
        out_specs=[out, out],
        out_shape=[jax.ShapeDtypeStruct((RECV, 2 * FF), F32)] * 2,
        compiler_params=pltpu.CompilerParams(vmem_limit_bytes=32 << 20),
        cost_estimate=pl.CostEstimate(
            flops=4 * RECV * WIDTH * 2 * FF, bytes_accessed=14000000, transcendentals=0
        ),
        name="forward",
    )(x_recv, gate_a, gate_b, up_a, up_b)


def backward_kernel(
    expert_ref, dy_ref, pre_gate_ref, pre_up_ref, gate_a, gate_b, up_a, up_b, down_a, down_b, out_ref
):
    turn = (((1,), (1,)), ((), ()))
    low = dy_ref[:, 0].reshape(-1, HALF)
    high = dy_ref[:, 1].reshape(-1, HALF)
    rows = low.shape[0]
    term = jnp.zeros((rows, 1), F32)
    pairs = []
    for i, down in enumerate((down_a, down_b)):
        d_hidden = lax.dot_general(
            low, down[:, :HALF], turn, preferred_element_type=F32
        ) + lax.dot_general(high, down[:, HALF:], turn, preferred_element_type=F32)
        pre_gate = pre_gate_ref[:, i * FF : (i + 1) * FF]
        pre_up = pre_up_ref[:, i * FF : (i + 1) * FF]
        sig = jax.nn.sigmoid(pre_gate)
        act = pre_gate * sig
        term = term + jnp.sum(act * pre_up * d_hidden, axis=1, keepdims=True)
        pairs.append(
            (
                (d_hidden * pre_up * sig * (1.0 + pre_gate * (1.0 - sig))).astype(BF16),
                (d_hidden * act).astype(BF16),
            )
        )
    for h in range(2):
        span = slice(h * HALF, (h + 1) * HALF)
        total = jnp.zeros((rows, HALF), F32)
        for (d_gate, d_up), gate, up in zip(pairs, (gate_a, gate_b), (up_a, up_b)):
            total = total + lax.dot_general(d_gate, gate[span, :], turn, preferred_element_type=F32)
            total = total + lax.dot_general(d_up, up[span, :], turn, preferred_element_type=F32)
        out_ref[:, h, :, :HALF] = total.astype(BF16).reshape(-1, SLOTS, HALF)
    lane = lax.broadcasted_iota(jnp.int32, (rows, META), 1)
    terms = jnp.where(lane == expert_ref[0], term, 0.0).astype(BF16).reshape(-1, SLOTS, META)
    out_ref[:, 0, :, HALF:] = terms
    out_ref[:, 1, :, HALF:] = terms


def backward(expert, dy_recv, pre_gate, pre_up, gate_a, gate_b, up_a, up_b, down_a, down_b):
    steps = 4
    weight = pl.BlockSpec((WIDTH, FF), lambda i, s: (0, 0))
    down = pl.BlockSpec((FF, WIDTH), lambda i, s: (0, 0))
    pre = pl.BlockSpec((RECV // steps, 2 * FF), lambda i, s: (i, 0))
    return pl.pallas_call(
        backward_kernel,
        grid_spec=pltpu.PrefetchScalarGridSpec(
            num_scalar_prefetch=1,
            grid=(steps,),
            in_specs=[
                pl.BlockSpec((16 // steps, 2, SLOTS, HALF), lambda i, s: (i, 0, 0, 0)),
                pre,
                pre,
                weight,
                weight,
                weight,
                weight,
                down,
                down,
            ],
            out_specs=pl.BlockSpec((16 // steps, 2, SLOTS, HALF + META), lambda i, s: (i, 0, 0, 0)),
        ),
        out_shape=jax.ShapeDtypeStruct((16, 2, SLOTS, HALF + META), BF16),
        compiler_params=pltpu.CompilerParams(vmem_limit_bytes=40 << 20),
        cost_estimate=pl.CostEstimate(
            flops=6 * RECV * WIDTH * 2 * FF, bytes_accessed=20000000, transcendentals=RECV * 768
        ),
        name="backward",
    )(expert, dy_recv, pre_gate, pre_up, gate_a, gate_b, up_a, up_b, down_a, down_b)


def combine_kernel(turned_ref, pick_rank_ref, pick_gate_ref, rank_ref, back_ref, out_ref):
    turned = turned_ref[...].astype(BF16)
    rank = jnp.dot(turned, pick_rank_ref[...], preferred_element_type=F32)
    gate = jnp.dot(turned, pick_gate_ref[...], preferred_element_type=F32)
    hit = rank == rank_ref[0:1, :]
    back = back_ref[...].reshape(ROWS, HALF + META)
    weighted = jnp.where(hit, gate, 0.0).astype(BF16)
    plain = jnp.where(hit, 1.0, 0.0).astype(BF16)
    out_ref[:, :HALF] = jnp.dot(weighted, back[:, :HALF], preferred_element_type=F32).astype(BF16)
    out_ref[:, HALF:] = jnp.dot(plain, back[:, HALF:], preferred_element_type=F32).astype(BF16)


def combine(turned, tables, back):
    steps = 4
    pick = pl.BlockSpec((128, ROWS), lambda i: (0, 0))
    return pl.pallas_call(
        combine_kernel,
        grid=(steps,),
        in_specs=[
            pl.BlockSpec((COL // steps, 128), lambda i: (i, 0)),
            pick,
            pick,
            pl.BlockSpec((8, ROWS), lambda i: (0, 0)),
            pl.BlockSpec((GROUPS, SLOTS, HALF + META), lambda i: (0, 0, 0)),
        ],
        out_specs=pl.BlockSpec((COL // steps, HALF + META), lambda i: (i, 0)),
        out_shape=jax.ShapeDtypeStruct((COL, HALF + META), BF16),
        compiler_params=pltpu.CompilerParams(vmem_limit_bytes=40 << 20),
        cost_estimate=pl.CostEstimate(
            flops=2 * ROWS * COL * (HALF + 3 * META), bytes_accessed=6000000, transcendentals=0
        ),
        name="combine",
    )(turned, *tables, back)


def on_device(tokens, grad_out, router_weight, expert_ids, gate_fixed, w_gate, w_up, w_down):
    z = lax.axis_index("z")
    yl = lax.axis_index("yl")
    owner = ((z * 2 + lax.axis_index("yh")) * 4 + lax.axis_index("x")) * 2 + yl

    def own_half(block):
        whole = lax.ppermute(block[0], ("c", "yl"), [(0, 0), (1, 2), (2, 1), (3, 3)])
        return whole, lax.ppermute(whole, "c", [(0, 1), (1, 0)])

    gate_a, gate_b = own_half(w_gate)
    up_a, up_b = own_half(w_up)
    down_a, down_b = own_half(w_down)

    ids = expert_ids.astype(BF16)
    high = (gate_fixed // 256).astype(BF16)
    low = (gate_fixed % 256).astype(BF16)
    blank = jnp.zeros((TOK, META - 3 * TOPK), BF16)
    x_half = lax.dynamic_slice_in_dim(tokens, yl * HALF, HALF, 1)
    dy_half = lax.dynamic_slice_in_dim(grad_out, yl * HALF, HALF, 1)
    x_col = lax.all_gather(
        jnp.concatenate([x_half, ids, high, low, blank], axis=1), "z", axis=0, tiled=True
    )
    dy_col = lax.all_gather(dy_half, "z", axis=0, tiled=True)

    rank, turned, counts = route(z.reshape(1).astype(jnp.int32), x_col)
    load = jnp.sum(lax.all_gather(counts[0:1], ("yh", "x", "c"), axis=0, tiled=True), axis=0)
    x_recv = lax.all_to_all(dispatch(rank, x_col), PLANE, split_axis=0, concat_axis=0, tiled=True)
    dy_recv = lax.all_to_all(dispatch(rank, dy_col), PLANE, split_axis=0, concat_axis=0, tiled=True)
    x_recv = x_recv.reshape(16, 2, SLOTS, HALF)
    dy_recv = dy_recv.reshape(16, 2, SLOTS, HALF)
    pre_gate, pre_up = forward(x_recv, gate_a, gate_b, up_a, up_b)
    grads = backward(
        owner.reshape(1).astype(jnp.int32),
        dy_recv,
        pre_gate,
        pre_up,
        gate_a,
        gate_b,
        up_a,
        up_b,
        down_a,
        down_b,
    )
    back = lax.all_to_all(
        grads.reshape(GROUPS, SLOTS, HALF + META), PLANE, split_axis=0, concat_axis=0, tiled=True
    )
    partial = combine(turned, slot_tables(), back)
    parts = lax.all_to_all(
        partial.reshape(16, TOK // 2, HALF + META), ("z", "yl"), split_axis=0, concat_axis=0, tiled=True
    ).reshape(Z, 2, TOK // 2, HALF + META)
    summed = jnp.sum(parts.astype(F32), axis=0)
    expert_grad = jnp.concatenate([summed[0, :, :HALF], summed[1, :, :HALF]], axis=1)
    own_ids = lax.dynamic_slice_in_dim(expert_ids, yl * (TOK // 2), TOK // 2, 0)
    chosen = own_ids[:, :, None] == jnp.arange(EXPERTS, dtype=jnp.int32)[None, None, :]
    d_gate = jnp.sum(jnp.where(chosen, summed[0, :, None, HALF:], 0.0), axis=2)

    own_tokens = lax.dynamic_slice_in_dim(tokens, yl * (TOK // 2), TOK // 2, 0)
    logits = jnp.dot(own_tokens, router_weight, preferred_element_type=F32)
    probs = jax.nn.softmax(logits, axis=1)
    share = load * EXPERTS / (EXPERTS * TOK * TOPK)
    d_logits = EXPERTS * probs * (
        share[None, :] - jnp.sum(probs * share[None, :], axis=1, keepdims=True)
    )
    router_back = lax.dot_general(
        d_logits.astype(BF16), router_weight, (((1,), (1,)), ((), ())), preferred_element_type=F32
    )
    grad_tokens = (expert_grad + router_back).astype(BF16)
    return grad_tokens, d_gate, d_logits


def solution(mesh):
    fine = Mesh(mesh.devices.reshape(8, 2, 4, 2, 2), ("z", "yh", "x", "c", "yl"))
    tok = ("z", "yh", "x", "c")
    return jax.shard_map(
        on_device,
        mesh=fine,
        in_specs=(
            P(tok, None),
            P(tok, None),
            P(),
            P(tok, None),
            P(tok, None),
            P(tok, None, "yl"),
            P(tok, None, "yl"),
            P(tok, "yl", None),
        ),
        out_specs=(
            P(tok + ("yl",), None),
            P(tok + ("yl",), None),
            P(tok + ("yl",), None),
        ),
        check_vma=False,
    )
```

```python
import jax
import jax.numpy as jnp
import numpy as np
from jax import lax
from jax.experimental import pallas as pl
from jax.experimental.pallas import tpu as pltpu
from jax.sharding import Mesh
from jax.sharding import PartitionSpec as P

EXPERTS = 128
Z = 8
PLANE_EXPERTS = 16
COLUMNS = 16
TOK = 128
COL = Z * TOK
WIDTH = 2048
HALF = 1024
QUARTERS = 4
QWIDTH = WIDTH // QUARTERS
META = 128
SHARE = 6
SLOTS = Z * SHARE
GROUPS = 32
ROWS = GROUPS * SLOTS
RECV = COLUMNS * SLOTS
PIECE = QUARTERS * SHARE
BACK = EXPERTS * PIECE
FF = 384
HID = 2 * FF
TOPK = 8
F32 = jnp.float32
BF16 = jnp.bfloat16
PLANE = ("yh", "x", "c", "yl")
SAME_SPLIT = ("z", "yh", "x", "c")
TURN = (((1,), (1,)), ((), ()))
OFFSETS = (0, -1, 1, -2, 2, -3, 3, 4)
CHUNKS = len(OFFSETS) + 1
MIB = 1 << 20


def turn_rows():
    pair, quarter, source, slot = np.meshgrid(
        np.arange(2), np.arange(QUARTERS), np.arange(Z), np.arange(SHARE), indexing="ij"
    )
    have = (pair * QUARTERS + quarter) * SLOTS + source * SHARE + slot
    want = ((source * 2 + pair) * QUARTERS + quarter) * SHARE + slot
    table = np.zeros((2 * QUARTERS * SLOTS,) * 2, np.float32)
    table[want.reshape(-1), have.reshape(-1)] = 1.0
    return jnp.asarray(table, BF16)


def term_tables():
    row = np.arange(RECV)
    column, source, slot = row // SLOTS, row % SLOTS // SHARE, row % SHARE
    to_lane = np.zeros((RECV, 128), np.float32)
    to_lane[row, column * SHARE + slot] = 1.0
    to_source = np.zeros((Z, RECV), np.float32)
    to_source[source, row] = 1.0
    return jnp.asarray(to_source, BF16), jnp.asarray(to_lane, BF16)


def place_tables():
    lane = np.arange(BACK)
    spread = (np.arange(EXPERTS)[:, None] == lane[None, :] // PIECE).astype(np.float32)
    quarter, slot = lane % PIECE // SHARE, lane % SHARE
    wanted = np.where(quarter[None, :] == np.arange(8)[:, None], slot[None, :], -9.0)
    return jnp.asarray(spread, BF16), jnp.asarray(wanted, F32)


def whole(shape):
    return pl.BlockSpec(shape, lambda *_: (0,) * len(shape))


def gather_place(code_ref, place):
    slot = lax.broadcasted_iota(jnp.int32, (SLOTS, COL), 0).astype(F32)
    for g in range(GROUPS):
        expert = (g // 4) * 2 + g % 2
        first = ((g // 2) % 2) * SLOTS
        hit = slot + float(first) == code_ref[expert : expert + 1, :]
        place[g * SLOTS : (g + 1) * SLOTS, :] = jnp.where(hit, 1.0, 0.0).astype(BF16)


def move_rows(chunk_refs, place, out_ref):
    rows = jnp.concatenate([ref[...] for ref in chunk_refs], axis=0)
    part = jnp.dot(place[...], rows, preferred_element_type=F32)
    out_ref[...] = part.astype(BF16).reshape(out_ref.shape)


def first_kernel(plane_ref, *refs):
    metas, chunks = refs[:CHUNKS], refs[CHUNKS : 2 * CHUNKS]
    out_ref, code_ref, count_ref, place, code_all = refs[2 * CHUNKS :]

    @pl.when(pl.program_id(0) == 0)
    def _():
        plane = plane_ref[0]
        turned = jnp.concatenate([ref[...] for ref in metas], axis=0).astype(F32).T
        expert = lax.broadcasted_iota(jnp.int32, (EXPERTS, COL), 0).astype(F32)
        member = jnp.zeros((EXPERTS, COL), F32)
        for k in range(TOPK):
            member = member + jnp.where(turned[k : k + 1, :] == expert, 1.0, 0.0)
        row = lax.broadcasted_iota(jnp.int32, (TOK, TOK), 0)
        column = lax.broadcasted_iota(jnp.int32, (TOK, TOK), 1)
        before = jnp.where(row < column, 1.0, 0.0).astype(BF16)
        low = member.astype(BF16)
        for i, offset in enumerate(OFFSETS):
            source = lax.rem(plane + (offset + Z), Z)
            base = (source * SHARE).astype(F32)
            span = slice(i * TOK, (i + 1) * TOK)
            rank = jnp.dot(low[:, span], before, preferred_element_type=F32)
            code = rank + base + jnp.where(rank >= SHARE, float(SLOTS - SHARE), 0.0)
            code_all[:, span] = jnp.where(member[:, span] > 0.0, code, -1.0)
        first = pl.multiple_of(plane * PLANE_EXPERTS, PLANE_EXPERTS)
        code_ref[...] = code_all[pl.ds(first, PLANE_EXPERTS), :]
        count_ref[...] = lax.dot_general(
            jnp.ones((8, COL), BF16), low, TURN, preferred_element_type=F32
        )
        gather_place(code_ref, place)

    move_rows(chunks, place, out_ref)


def second_kernel(code_ref, *refs):
    chunks, (out_ref, place) = refs[:CHUNKS], refs[CHUNKS:]

    @pl.when(pl.program_id(0) == 0)
    def _():
        gather_place(code_ref, place)

    move_rows(chunks, place, out_ref)


DISPATCH_COST = pl.CostEstimate(
    flops=2 * ROWS * COL * HALF, bytes_accessed=5500000, transcendentals=0
)


def first_dispatch(plane, chunks):
    block = 256
    return pl.pallas_call(
        first_kernel,
        grid_spec=pltpu.PrefetchScalarGridSpec(
            num_scalar_prefetch=1,
            grid=(HALF // block,),
            in_specs=[
                pl.BlockSpec((chunk.shape[0], META), lambda i, s: (0, HALF // META))
                for chunk in chunks
            ]
            + [pl.BlockSpec((chunk.shape[0], block), lambda i, s: (0, i)) for chunk in chunks],
            out_specs=[
                pl.BlockSpec((GROUPS, SLOTS, block), lambda i, s: (0, 0, i)),
                whole((PLANE_EXPERTS, COL)),
                whole((8, EXPERTS)),
            ],
            scratch_shapes=[pltpu.VMEM((ROWS, COL), BF16), pltpu.VMEM((EXPERTS, COL), F32)],
        ),
        out_shape=[
            jax.ShapeDtypeStruct((GROUPS, SLOTS, HALF), BF16),
            jax.ShapeDtypeStruct((PLANE_EXPERTS, COL), F32),
            jax.ShapeDtypeStruct((8, EXPERTS), F32),
        ],
        compiler_params=pltpu.CompilerParams(vmem_limit_bytes=56 * MIB),
        cost_estimate=DISPATCH_COST,
        name="route_x",
    )(plane, *chunks, *chunks)


def second_dispatch(code, chunks):
    block = 256
    return pl.pallas_call(
        second_kernel,
        grid=(HALF // block,),
        in_specs=[whole((PLANE_EXPERTS, COL))]
        + [pl.BlockSpec((chunk.shape[0], block), lambda i: (0, i)) for chunk in chunks],
        out_specs=pl.BlockSpec((GROUPS, SLOTS, block), lambda i: (0, 0, i)),
        out_shape=jax.ShapeDtypeStruct((GROUPS, SLOTS, HALF), BF16),
        scratch_shapes=[pltpu.VMEM((ROWS, COL), BF16)],
        compiler_params=pltpu.CompilerParams(vmem_limit_bytes=56 * MIB),
        cost_estimate=DISPATCH_COST,
        name="dispatch",
    )(code, *chunks)


def forward_kernel(x_ref, gate_a, gate_b, up_a, up_b, hidden_ref, act_ref, slope_ref):
    low = x_ref[:, 0].reshape(-1, HALF)
    high = x_ref[:, 1].reshape(-1, HALF)
    for i, (gate, up) in enumerate(((gate_a, up_a), (gate_b, up_b))):
        span = slice(i * FF, (i + 1) * FF)
        pre_gate = jnp.dot(low, gate[:HALF, :], preferred_element_type=F32) + jnp.dot(
            high, gate[HALF:, :], preferred_element_type=F32
        )
        pre_up = jnp.dot(low, up[:HALF, :], preferred_element_type=F32) + jnp.dot(
            high, up[HALF:, :], preferred_element_type=F32
        )
        sig = jax.nn.sigmoid(pre_gate)
        act = pre_gate * sig
        hidden_ref[:, span] = (act * pre_up).astype(BF16)
        act_ref[:, span] = act.astype(BF16)
        slope_ref[:, span] = (pre_up * sig * (1.0 + pre_gate * (1.0 - sig))).astype(BF16)


def forward(x_recv, gate_a, gate_b, up_a, up_b):
    steps = 2
    out = pl.BlockSpec((RECV // steps, HID), lambda i: (i, 0))
    return pl.pallas_call(
        forward_kernel,
        grid=(steps,),
        in_specs=[pl.BlockSpec((COLUMNS // steps, 2, SLOTS, HALF), lambda i: (i, 0, 0, 0))]
        + [whole((WIDTH, FF))] * 4,
        out_specs=[out] * 3,
        out_shape=[jax.ShapeDtypeStruct((RECV, HID), BF16)] * 3,
        compiler_params=pltpu.CompilerParams(vmem_limit_bytes=56 * MIB),
        cost_estimate=pl.CostEstimate(
            flops=4 * RECV * WIDTH * HID, bytes_accessed=14000000, transcendentals=RECV * HID
        ),
        name="forward",
    )(x_recv, gate_a, gate_b, up_a, up_b)


def backward_kernel(
    dy_hbm, hidden_hbm, act_hbm, slope_hbm, gate_a, gate_b, up_a, up_b, down_a, down_b,
    turn_ref, source_ref, lane_ref, out_ref, term_ref,
    dy, hidden, act, slope, ins, down, d_pre, grads, sems,
):
    copies = [
        pltpu.make_async_copy(dy_hbm.at[:, 0], dy.at[:, :, pl.ds(0, HALF)], sems.at[0]),
        pltpu.make_async_copy(dy_hbm.at[:, 1], dy.at[:, :, pl.ds(HALF, HALF)], sems.at[1]),
        pltpu.make_async_copy(down_a, down.at[pl.ds(0, FF)], sems.at[2]),
        pltpu.make_async_copy(down_b, down.at[pl.ds(FF, FF)], sems.at[3]),
        pltpu.make_async_copy(hidden_hbm, hidden, sems.at[4]),
        pltpu.make_async_copy(act_hbm, act, sems.at[5]),
        pltpu.make_async_copy(slope_hbm, slope, sems.at[6]),
    ]
    for i, weight in enumerate((gate_a, up_a, gate_b, up_b)):
        copies.append(
            pltpu.make_async_copy(weight, ins.at[:, pl.ds(i * FF, FF)], sems.at[7 + i])
        )
    for copy in copies:
        copy.start()
    copies[0].wait()
    copies[1].wait()
    copies[2].wait()
    term = jnp.zeros((RECV, 1), F32)
    rows = dy[...].reshape(RECV, WIDTH)
    for i in range(2):
        span = slice(i * FF, (i + 1) * FF)
        if i == 1:
            copies[3].wait()
        d_hidden = lax.dot_general(rows, down[span, :], TURN, preferred_element_type=F32)
        if i == 0:
            copies[4].wait()
            copies[5].wait()
            copies[6].wait()
        term = term + jnp.sum(d_hidden * hidden[:, span].astype(F32), axis=1, keepdims=True)
        first = 2 * i * FF
        d_pre[:, first : first + FF] = (d_hidden * slope[:, span].astype(F32)).astype(BF16)
        d_pre[:, first + FF : first + 2 * FF] = (d_hidden * act[:, span].astype(F32)).astype(BF16)
    spread = jnp.where(lane_ref[...] > 0.0, term, 0.0).astype(BF16)
    term_ref[...] = jnp.dot(source_ref[...], spread, preferred_element_type=F32)
    for copy in copies[7:]:
        copy.wait()
    for q in range(QUARTERS):
        span = slice(q * QWIDTH, (q + 1) * QWIDTH)
        grads[:, span] = lax.dot_general(
            d_pre[...], ins[span, :], TURN, preferred_element_type=F32
        ).astype(BF16)
    for pair in range(COLUMNS // 2):
        pieces = [
            grads[(2 * pair + j) * SLOTS : (2 * pair + j + 1) * SLOTS, q * QWIDTH : (q + 1) * QWIDTH]
            for j in range(2)
            for q in range(QUARTERS)
        ]
        moved = jnp.dot(
            turn_ref[...], jnp.concatenate(pieces, axis=0), preferred_element_type=F32
        ).astype(BF16)
        out_ref[:, pair * 2 * PIECE : (pair + 1) * 2 * PIECE, :] = moved.reshape(
            Z, 2 * PIECE, QWIDTH
        )


def backward(dy_recv, hidden, act, slope, gate_a, gate_b, up_a, up_b, down_a, down_b):
    far = pl.BlockSpec(memory_space=pl.ANY)
    near = pl.BlockSpec(memory_space=pltpu.VMEM)
    return pl.pallas_call(
        backward_kernel,
        in_specs=[far] * 10 + [near] * 3,
        out_specs=[near, near],
        out_shape=[
            jax.ShapeDtypeStruct((Z, COLUMNS * PIECE, QWIDTH), BF16),
            jax.ShapeDtypeStruct((Z, 128), F32),
        ],
        scratch_shapes=[
            pltpu.VMEM((COLUMNS, SLOTS, WIDTH), BF16),
            pltpu.VMEM((RECV, HID), BF16),
            pltpu.VMEM((RECV, HID), BF16),
            pltpu.VMEM((RECV, HID), BF16),
            pltpu.VMEM((WIDTH, 2 * HID), BF16),
            pltpu.VMEM((HID, WIDTH), BF16),
            pltpu.VMEM((RECV, 2 * HID), BF16),
            pltpu.VMEM((RECV, WIDTH), BF16),
            pltpu.SemaphoreType.DMA((11,)),
        ],
        compiler_params=pltpu.CompilerParams(vmem_limit_bytes=56 * MIB),
        cost_estimate=pl.CostEstimate(
            flops=6 * RECV * WIDTH * HID, bytes_accessed=20000000, transcendentals=0
        ),
        name="backward",
    )(
        dy_recv, hidden, act, slope, gate_a, gate_b, up_a, up_b, down_a, down_b,
        turn_rows(), *term_tables(),
    )


def place_kernel(half_ref, ids_ref, gates_ref, spread_ref, wanted_ref, place_ref, code_ref):
    lane = lax.broadcasted_iota(jnp.int32, (TOK, EXPERTS), 1)
    core = (lane % 2).astype(F32)
    expert = lane - lane % 2 + half_ref[0]
    member = jnp.zeros((TOK, EXPERTS), F32)
    gate = jnp.zeros((TOK, EXPERTS), F32)
    for k in range(TOPK):
        same = ids_ref[:, k : k + 1] == expert
        value = gates_ref[:, k : k + 1].astype(F32) * (1.0 / 65536.0)
        member = member + jnp.where(same, 1.0, 0.0)
        gate = gate + jnp.where(same, value, 0.0)
    row = lax.broadcasted_iota(jnp.int32, (TOK, TOK), 0)
    column = lax.broadcasted_iota(jnp.int32, (TOK, TOK), 1)
    before = jnp.where(column < row, 1.0, 0.0).astype(BF16)
    rank = jnp.dot(before, member.astype(BF16), preferred_element_type=F32)
    upper = jnp.where(rank >= SHARE, 1.0, 0.0)
    code = jnp.where((member > 0.0) & (upper == core), rank - SHARE * upper, -1.0)
    code_ref[...] = code
    code_wide = jnp.dot(code.astype(BF16), spread_ref[...], preferred_element_type=F32)
    gate_wide = jnp.dot(gate.astype(BF16), spread_ref[...], preferred_element_type=F32)
    for q in range(QUARTERS):
        hit = code_wide == wanted_ref[q : q + 1, :]
        place_ref[q * TOK : (q + 1) * TOK, :] = jnp.where(hit, gate_wide, 0.0).astype(BF16)


def make_place(half, ids, gates):
    return pl.pallas_call(
        place_kernel,
        grid_spec=pltpu.PrefetchScalarGridSpec(
            num_scalar_prefetch=1,
            grid=(1,),
            in_specs=[
                whole((TOK, TOPK)),
                whole((TOK, TOPK)),
                whole((EXPERTS, BACK)),
                whole((8, BACK)),
            ],
            out_specs=[whole((QUARTERS * TOK, BACK)), whole((TOK, EXPERTS))],
        ),
        out_shape=[
            jax.ShapeDtypeStruct((QUARTERS * TOK, BACK), BF16),
            jax.ShapeDtypeStruct((TOK, EXPERTS), F32),
        ],
        compiler_params=pltpu.CompilerParams(vmem_limit_bytes=40 * MIB),
        cost_estimate=pl.CostEstimate(flops=300000000, bytes_accessed=4000000, transcendentals=0),
        name="place",
    )(half, ids, gates, *place_tables())


def terms_kernel(where_ref, code_ref, ids_ref, *refs):
    parts, (mine_ref, theirs_ref, every, out) = refs[:Z], refs[Z:]
    half = where_ref[2]
    for distance, part in enumerate(parts):
        source = lax.rem(where_ref[1] + (Z - distance), Z)
        first = pl.multiple_of(source * COLUMNS, COLUMNS)
        every[pl.ds(first, COLUMNS), :] = part[...]
    slot = lax.broadcasted_iota(jnp.int32, (8, 128), 0)
    lane = lax.broadcasted_iota(jnp.int32, (8, 128), 1)
    pick = jnp.where((lane == slot + where_ref[0]) & (slot < SHARE), 1.0, 0.0)
    term = lax.dot_general(
        pick.astype(BF16), every[...].astype(BF16), TURN, preferred_element_type=F32
    )
    found = jnp.zeros((TOK, EXPERTS), F32)
    for s in range(SHARE):
        found = found + jnp.where(code_ref[...] == float(s), term[s : s + 1, :], 0.0)
    column = lax.broadcasted_iota(jnp.int32, (TOK, EXPERTS), 1)
    expert = column - column % 2 + half
    total = jnp.zeros((TOK, 128), F32)
    for k in range(TOPK):
        hit = jnp.where(ids_ref[:, k : k + 1] == expert, found, 0.0)
        total = jnp.where(column == k, jnp.sum(hit, axis=1, keepdims=True), total)
    out[...] = total
    rows = TOK // 2
    mine_ref[...] = out[pl.ds(pl.multiple_of(half * rows, rows), rows), :]
    theirs_ref[...] = out[pl.ds(pl.multiple_of((1 - half) * rows, rows), rows), :]


def own_terms(where, parts, code, ids):
    near = pl.BlockSpec(memory_space=pltpu.VMEM)
    return pl.pallas_call(
        terms_kernel,
        in_specs=[pl.BlockSpec(memory_space=pltpu.SMEM)] + [near] * (2 + Z),
        out_specs=[near, near],
        out_shape=[jax.ShapeDtypeStruct((TOK // 2, 128), F32)] * 2,
        scratch_shapes=[pltpu.VMEM((EXPERTS, 128), F32), pltpu.VMEM((TOK, 128), F32)],
        cost_estimate=pl.CostEstimate(flops=1000000, bytes_accessed=300000, transcendentals=0),
        name="terms",
    )(where, code, ids, *parts)


def combine_kernel(
    half_ref, place_hbm, back_hbm, mine_ref, theirs_ref, place, back, total, sems
):
    depth = BACK // STEPS
    copies = []
    for i in range(STEPS):
        span = pl.ds(i * depth, depth)
        copies.append(
            (
                pltpu.make_async_copy(place_hbm.at[:, span], place.at[:, span], sems.at[2 * i]),
                pltpu.make_async_copy(back_hbm.at[span], back.at[span], sems.at[2 * i + 1]),
            )
        )
    for pair in copies:
        for copy in pair:
            copy.start()
    for i, pair in enumerate(copies):
        for copy in pair:
            copy.wait()
        span = slice(i * depth, (i + 1) * depth)
        part = jnp.dot(place[:, span], back[span, :], preferred_element_type=F32)
        total[...] = part if i == 0 else total[...] + part
    rows = TOK // 2
    for q in range(QUARTERS):
        span = slice(q * QWIDTH, (q + 1) * QWIDTH)
        own = pl.multiple_of(q * TOK + half_ref[0] * rows, rows)
        other = pl.multiple_of(q * TOK + (1 - half_ref[0]) * rows, rows)
        theirs_ref[:, span] = total[pl.ds(other, rows), :].astype(BF16)
        mine_ref[:, span] = total[pl.ds(own, rows), :]


STEPS = 4


def combine(half, place, back):
    near = pl.BlockSpec(memory_space=pltpu.VMEM)
    return pl.pallas_call(
        combine_kernel,
        in_specs=[
            pl.BlockSpec(memory_space=pltpu.SMEM),
            pl.BlockSpec(memory_space=pl.ANY),
            pl.BlockSpec(memory_space=pl.ANY),
        ],
        out_specs=[near, near],
        out_shape=[
            jax.ShapeDtypeStruct((TOK // 2, WIDTH), F32),
            jax.ShapeDtypeStruct((TOK // 2, WIDTH), BF16),
        ],
        scratch_shapes=[
            pltpu.VMEM((QUARTERS * TOK, BACK), BF16),
            pltpu.VMEM((BACK, QWIDTH), BF16),
            pltpu.VMEM((QUARTERS * TOK, QWIDTH), F32),
            pltpu.SemaphoreType.DMA((2 * STEPS,)),
        ],
        compiler_params=pltpu.CompilerParams(vmem_limit_bytes=56 * MIB),
        cost_estimate=pl.CostEstimate(
            flops=2 * QUARTERS * TOK * BACK * QWIDTH, bytes_accessed=8000000, transcendentals=0
        ),
        name="combine",
    )(half, place, back)


def on_device(tokens, grad_out, router_weight, expert_ids, gate_fixed, w_gate, w_up, w_down):
    z = lax.axis_index("z")
    yl = lax.axis_index("yl")
    c = lax.axis_index("c")
    column = (lax.axis_index("yh") * 4 + lax.axis_index("x")) * 2 + c
    at_home = c == yl
    half_index = yl.reshape(1).astype(jnp.int32)

    def cross(block):
        return lax.ppermute(block, ("c", "yl"), [(1, 2), (2, 1)])

    def other_core(block):
        return lax.ppermute(block, "c", [(0, 1), (1, 0)])

    def half_columns(block):
        return lax.dynamic_slice_in_dim(block, yl * HALF, HALF, 1)

    def exchange(block):
        return lax.all_to_all(block, PLANE, split_axis=0, concat_axis=0, tiled=True)

    def ring(block):
        ahead = [(i, (i + 1) % Z) for i in range(Z)]
        behind = [(i, (i - 1) % Z) for i in range(Z)]
        found, left, right = [block], block, block
        for step in range(4):
            if step == 3:
                left, right = left[: TOK // 2], right[TOK // 2 :]
            left, right = lax.ppermute(left, "z", ahead), lax.ppermute(right, "z", behind)
            found += [left, right]
        return found

    gate_c, up_c, down_c = cross(w_gate[0]), cross(w_up[0]), cross(w_down[0])
    blank = jnp.zeros((TOK, META - TOPK), BF16)
    x_chunks = ring(
        jnp.concatenate([half_columns(tokens), expert_ids.astype(BF16), blank], axis=1)
    )
    dy_half, x_chunks[-1] = lax.optimization_barrier((half_columns(grad_out), x_chunks[-1]))
    x_send, code, counts = first_dispatch(z.reshape(1).astype(jnp.int32), x_chunks)
    dy_chunks = ring(dy_half)
    x_send, gate_c, up_c, down_c = lax.optimization_barrier((x_send, gate_c, up_c, down_c))
    gate_a = jnp.where(at_home, w_gate[0], gate_c)
    up_a = jnp.where(at_home, w_up[0], up_c)
    x_recv = exchange(x_send)
    gate_b, up_b = other_core(gate_a), other_core(up_a)
    dy_send = second_dispatch(code, dy_chunks)
    down_a = jnp.where(at_home, w_down[0], down_c)
    dy_recv = exchange(dy_send)
    down_b = other_core(down_a)
    hidden, act, slope = forward(
        x_recv.reshape(COLUMNS, 2, SLOTS, HALF), gate_a, gate_b, up_a, up_b
    )
    grads, terms = backward(
        dy_recv.reshape(COLUMNS, 2, SLOTS, HALF),
        hidden, act, slope, gate_a, gate_b, up_a, up_b, down_a, down_b,
    )
    back = lax.all_to_all(
        grads.reshape(BACK, QWIDTH), SAME_SPLIT, split_axis=0, concat_axis=0, tiled=True
    )
    plane_news = lax.all_gather(
        jnp.concatenate([terms, counts], axis=0), ("yh", "x", "c"), axis=0, tiled=False
    )
    load = plane_news[:, Z].sum(axis=0)

    def terms_for(distance):
        return lax.dynamic_index_in_dim(plane_news, (z + distance) % Z, 1, keepdims=False)

    found_terms = [terms_for(0)] + [
        lax.ppermute(terms_for(d), "z", [(i, (i + d) % Z) for i in range(Z)]) for d in range(1, Z)
    ]

    half_rows = TOK // 2
    place, own_code = make_place(half_index, expert_ids, gate_fixed)
    swap = [(0, 1), (1, 0)]

    own_tokens = lax.dynamic_slice_in_dim(tokens, yl * half_rows, half_rows, 0)
    logits = jnp.dot(own_tokens, router_weight, preferred_element_type=F32)
    probs = jax.nn.softmax(logits, axis=1)
    share = load * EXPERTS / (EXPERTS * TOK * TOPK)
    d_logits = EXPERTS * probs * (
        share[None, :] - jnp.sum(probs * share[None, :], axis=1, keepdims=True)
    )
    router_back = lax.dot_general(
        d_logits.astype(BF16), router_weight, TURN, preferred_element_type=F32
    )

    back, router_back, place = lax.optimization_barrier((back, router_back, place))
    mine, theirs = combine(half_index, place, back)
    theirs, found_terms = lax.optimization_barrier((theirs, found_terms))
    theirs = lax.ppermute(theirs, "yl", swap)
    where = jnp.stack([column * SHARE, z, yl]).astype(jnp.int32)
    d_mine, d_theirs = own_terms(where, found_terms, own_code, expert_ids)
    d_gate = (d_mine + lax.ppermute(d_theirs, "yl", swap))[:, :TOPK]
    grad_tokens = (mine + theirs.astype(F32) + router_back).astype(BF16)
    return grad_tokens, d_gate, d_logits


def solution(mesh):
    fine = Mesh(mesh.devices.reshape(8, 2, 4, 2, 2), ("z", "yh", "x", "c", "yl"))
    return jax.shard_map(
        on_device,
        mesh=fine,
        in_specs=(
            P(SAME_SPLIT, None),
            P(SAME_SPLIT, None),
            P(),
            P(SAME_SPLIT, None),
            P(SAME_SPLIT, None),
            P(SAME_SPLIT, None, "yl"),
            P(SAME_SPLIT, None, "yl"),
            P(SAME_SPLIT, "yl", None),
        ),
        out_specs=(
            P(SAME_SPLIT + ("yl",), None),
            P(SAME_SPLIT + ("yl",), None),
            P(SAME_SPLIT + ("yl",), None),
        ),
        check_vma=False,
    )
```

```python
import functools

import jax
import jax.numpy as jnp
import numpy as np
from jax import lax
from jax.experimental import pallas as pl
from jax.experimental.pallas import tpu as pltpu
from jax.sharding import Mesh
from jax.sharding import PartitionSpec as P

EXPERTS = 128
Z = 8
PLANE_EXPERTS = 16
COLUMNS = 16
TOK = 128
COL = Z * TOK
WIDTH = 2048
HALF = 1024
QUARTERS = 4
QWIDTH = WIDTH // QUARTERS
META = 128
SHARE = 6
SLOTS = Z * SHARE
GROUPS = 32
ROWS = GROUPS * SLOTS
RECV = COLUMNS * SLOTS
PIECE = QUARTERS * SHARE
BACK = EXPERTS * PIECE
FF = 384
HID = 2 * FF
TOPK = 8
F32 = jnp.float32
BF16 = jnp.bfloat16
PLANE = ("yh", "x", "c", "yl")
SAME_SPLIT = ("z", "yh", "x", "c")
TURN = (((1,), (1,)), ((), ()))
NEAR = (0, -1, 1, -2, 2, -3, 3)
FAR = (4,)
MIB = 1 << 20


def turn_rows():
    pair, quarter, source, slot = np.meshgrid(
        np.arange(2), np.arange(QUARTERS), np.arange(Z), np.arange(SHARE), indexing="ij"
    )
    have = (pair * QUARTERS + quarter) * SLOTS + source * SHARE + slot
    want = ((source * 2 + pair) * QUARTERS + quarter) * SHARE + slot
    table = np.zeros((2 * QUARTERS * SLOTS,) * 2, np.float32)
    table[want.reshape(-1), have.reshape(-1)] = 1.0
    return jnp.asarray(table, BF16)


def term_tables():
    row = np.arange(RECV)
    column, source, slot = row // SLOTS, row % SLOTS // SHARE, row % SHARE
    to_lane = np.zeros((RECV, 128), np.float32)
    to_lane[row, column * SHARE + slot] = 1.0
    to_source = np.zeros((Z, RECV), np.float32)
    to_source[source, row] = 1.0
    return jnp.asarray(to_source, BF16), jnp.asarray(to_lane, BF16)


def place_tables():
    lane = np.arange(BACK)
    spread = (np.arange(EXPERTS)[:, None] == lane[None, :] // PIECE).astype(np.float32)
    quarter, slot = lane % PIECE // SHARE, lane % SHARE
    wanted = np.where(quarter[None, :] == np.arange(8)[:, None], slot[None, :], -9.0)
    return jnp.asarray(spread, BF16), jnp.asarray(wanted, F32)


def whole(shape):
    return pl.BlockSpec(shape, lambda *_: (0,) * len(shape))


def slot_codes(plane, offsets, meta_refs, code_ref, count_ref, code_all):
    width = TOK * len(offsets)
    turned = jnp.concatenate([ref[...] for ref in meta_refs], axis=0).astype(F32).T
    expert = lax.broadcasted_iota(jnp.int32, (EXPERTS, width), 0).astype(F32)
    member = jnp.zeros((EXPERTS, width), F32)
    for k in range(TOPK):
        member = member + jnp.where(turned[k : k + 1, :] == expert, 1.0, 0.0)
    row = lax.broadcasted_iota(jnp.int32, (TOK, TOK), 0)
    column = lax.broadcasted_iota(jnp.int32, (TOK, TOK), 1)
    before = jnp.where(row < column, 1.0, 0.0).astype(BF16)
    low = member.astype(BF16)
    for i, offset in enumerate(offsets):
        source = lax.rem(plane + (offset + Z), Z)
        base = (source * SHARE).astype(F32)
        span = slice(i * TOK, (i + 1) * TOK)
        rank = jnp.dot(low[:, span], before, preferred_element_type=F32)
        code = rank + base + jnp.where(rank >= SHARE, float(SLOTS - SHARE), 0.0)
        code_all[:, span] = jnp.where(member[:, span] > 0.0, code, -1.0)
    first = pl.multiple_of(plane * PLANE_EXPERTS, PLANE_EXPERTS)
    code_ref[...] = code_all[pl.ds(first, PLANE_EXPERTS), :]
    count_ref[...] = lax.dot_general(
        jnp.ones((8, width), BF16), low, TURN, preferred_element_type=F32
    )


def gather_place(code_ref, place):
    slot = lax.broadcasted_iota(jnp.int32, (SLOTS, place.shape[1]), 0).astype(F32)
    for g in range(GROUPS):
        expert = (g // 4) * 2 + g % 2
        first = ((g // 2) % 2) * SLOTS
        hit = slot + float(first) == code_ref[expert : expert + 1, :]
        place[g * SLOTS : (g + 1) * SLOTS, :] = jnp.where(hit, 1.0, 0.0).astype(BF16)


def move_rows(chunk_refs, place, out_ref, before_ref=None):
    rows = jnp.concatenate([ref[...] for ref in chunk_refs], axis=0)
    part = jnp.dot(place[...], rows, preferred_element_type=F32)
    part = part.astype(BF16).reshape(out_ref.shape)
    out_ref[...] = part if before_ref is None else part + before_ref[...]


def route_kernel(offsets, count, more, plane_ref, *refs):
    metas, chunks, rest = refs[:count], refs[count : 2 * count], refs[2 * count :]
    before_ref = rest[0] if more else None
    out_ref, code_ref, count_ref, place, code_all = rest[more:]

    @pl.when(pl.program_id(0) == 0)
    def _():
        slot_codes(plane_ref[0], offsets, metas, code_ref, count_ref, code_all)
        gather_place(code_ref, place)

    move_rows(chunks, place, out_ref, before_ref)


def follow_kernel(count, more, plane_ref, code_ref, *refs):
    chunks, rest = refs[:count], refs[count:]
    before_ref = rest[0] if more else None
    out_ref, place = rest[more:]

    @pl.when(pl.program_id(0) == 0)
    def _():
        gather_place(code_ref, place)

    move_rows(chunks, place, out_ref, before_ref)


def dispatch(plane, offsets, chunks, before=None, code=None):
    block = 256
    count, more, width = len(chunks), int(before is not None), TOK * len(offsets)
    moved = pl.BlockSpec((GROUPS, SLOTS, block), lambda i, s: (0, 0, i))
    moved_shape = jax.ShapeDtypeStruct((GROUPS, SLOTS, HALF), BF16)
    meta_specs = [
        pl.BlockSpec((chunk.shape[0], META), lambda i, s: (0, HALF // META)) for chunk in chunks
    ]
    chunk_specs = [pl.BlockSpec((chunk.shape[0], block), lambda i, s: (0, i)) for chunk in chunks]
    tail = [before] if more else []
    place = pltpu.VMEM((ROWS, width), BF16)
    if code is None:
        kernel = functools.partial(route_kernel, offsets, count, more)
        operands = (*chunks, *chunks, *tail)
        in_specs = meta_specs + chunk_specs + [moved] * more
        out_specs = [moved, whole((PLANE_EXPERTS, width)), whole((8, EXPERTS))]
        out_shape = [
            moved_shape,
            jax.ShapeDtypeStruct((PLANE_EXPERTS, width), F32),
            jax.ShapeDtypeStruct((8, EXPERTS), F32),
        ]
        scratch = [place, pltpu.VMEM((EXPERTS, width), F32)]
    else:
        kernel = functools.partial(follow_kernel, count, more)
        operands = (code, *chunks, *tail)
        in_specs = [whole((PLANE_EXPERTS, width))] + chunk_specs + [moved] * more
        out_specs, out_shape, scratch = moved, moved_shape, [place]
    return pl.pallas_call(
        kernel,
        grid_spec=pltpu.PrefetchScalarGridSpec(
            num_scalar_prefetch=1,
            grid=(HALF // block,),
            in_specs=in_specs,
            out_specs=out_specs,
            scratch_shapes=scratch,
        ),
        out_shape=out_shape,
        compiler_params=pltpu.CompilerParams(vmem_limit_bytes=56 * MIB),
        cost_estimate=pl.CostEstimate(
            flops=2 * ROWS * width * HALF, bytes_accessed=5500000, transcendentals=0
        ),
        name="dispatch",
    )(plane, *operands)


def forward_kernel(x_ref, gate_a, gate_b, up_a, up_b, hidden_ref, act_ref, slope_ref):
    low = x_ref[:, 0].reshape(-1, HALF)
    high = x_ref[:, 1].reshape(-1, HALF)
    for i, (gate, up) in enumerate(((gate_a, up_a), (gate_b, up_b))):
        span = slice(i * FF, (i + 1) * FF)
        pre_gate = jnp.dot(low, gate[:HALF, :], preferred_element_type=F32) + jnp.dot(
            high, gate[HALF:, :], preferred_element_type=F32
        )
        pre_up = jnp.dot(low, up[:HALF, :], preferred_element_type=F32) + jnp.dot(
            high, up[HALF:, :], preferred_element_type=F32
        )
        sig = jax.nn.sigmoid(pre_gate)
        act = pre_gate * sig
        hidden_ref[:, span] = (act * pre_up).astype(BF16)
        act_ref[:, span] = act.astype(BF16)
        slope_ref[:, span] = (pre_up * sig * (1.0 + pre_gate * (1.0 - sig))).astype(BF16)


def forward(x_recv, gate_a, gate_b, up_a, up_b):
    steps = 2
    out = pl.BlockSpec((RECV // steps, HID), lambda i: (i, 0))
    return pl.pallas_call(
        forward_kernel,
        grid=(steps,),
        in_specs=[pl.BlockSpec((COLUMNS // steps, 2, SLOTS, HALF), lambda i: (i, 0, 0, 0))]
        + [whole((WIDTH, FF))] * 4,
        out_specs=[out] * 3,
        out_shape=[jax.ShapeDtypeStruct((RECV, HID), BF16)] * 3,
        compiler_params=pltpu.CompilerParams(vmem_limit_bytes=56 * MIB),
        cost_estimate=pl.CostEstimate(
            flops=4 * RECV * WIDTH * HID, bytes_accessed=14000000, transcendentals=RECV * HID
        ),
        name="forward",
    )(x_recv, gate_a, gate_b, up_a, up_b)


def backward_kernel(
    dy_hbm, hidden_hbm, act_hbm, slope_hbm, gate_a, gate_b, up_a, up_b, down_a, down_b, tail_a, tail_b,
    turn_ref, source_ref, lane_ref, out_hbm, term_ref,
    dy, hidden, act, slope, ins, down, d_pre, grads, out, in_sems, out_sems,
):
    cut = down_a.shape[0]
    plan = []
    for h in range(2):
        span = pl.ds(h * HALF, HALF)
        plan.append((dy_hbm.at[:, h], dy.at[:, :, span]))
        first = 0
        for block in (down_a, tail_a, down_b, tail_b):
            plan.append((block.at[:, span], down.at[pl.ds(first, cut), span]))
            first += cut
    plan += [(hidden_hbm, hidden), (act_hbm, act), (slope_hbm, slope)]
    for i, weight in enumerate((gate_a, up_a, gate_b, up_b)):
        plan.append((weight, ins.at[:, pl.ds(i * FF, FF)]))
    copies = [
        pltpu.make_async_copy(source, target, in_sems.at[i])
        for i, (source, target) in enumerate(plan)
    ]
    for copy in copies[:10]:
        copy.start()
    for copy in copies[:5]:
        copy.wait()
    for copy in copies[10:]:
        copy.start()
    rows = dy[:, :, :HALF].reshape(RECV, HALF)
    d_hidden = lax.dot_general(rows, down[:, :HALF], TURN, preferred_element_type=F32)
    for copy in copies[5:10]:
        copy.wait()
    rows = dy[:, :, HALF:].reshape(RECV, HALF)
    d_hidden = d_hidden + lax.dot_general(
        rows, down[:, HALF:], TURN, preferred_element_type=F32
    )
    for copy in copies[10:13]:
        copy.wait()
    term = jnp.sum(d_hidden * hidden[...].astype(F32), axis=1, keepdims=True)
    d_gate = (d_hidden * slope[...].astype(F32)).astype(BF16)
    d_up = (d_hidden * act[...].astype(F32)).astype(BF16)
    for i in range(2):
        span = slice(i * FF, (i + 1) * FF)
        first = 2 * i * FF
        d_pre[:, first : first + FF] = d_gate[:, span]
        d_pre[:, first + FF : first + 2 * FF] = d_up[:, span]
    spread = jnp.where(lane_ref[...] > 0.0, term, 0.0).astype(BF16)
    term_ref[...] = jnp.dot(source_ref[...], spread, preferred_element_type=F32)
    for copy in copies[13:]:
        copy.wait()
    for q in range(QUARTERS):
        part = lax.dot_general(
            d_pre[...],
            ins[q * QWIDTH : (q + 1) * QWIDTH, :],
            TURN,
            preferred_element_type=F32,
        )
        grads[:, q] = part.astype(BF16).reshape(COLUMNS, SLOTS, QWIDTH)
    sends = []
    for pair in range(COLUMNS // 2):
        piece = grads[2 * pair : 2 * pair + 2].reshape(2 * QUARTERS * SLOTS, QWIDTH)
        moved = jnp.dot(turn_ref[...], piece, preferred_element_type=F32).astype(BF16)
        span = pl.ds(pair * 2 * PIECE, 2 * PIECE)
        out[:, span, :] = moved.reshape(Z, 2 * PIECE, QWIDTH)
        send = pltpu.make_async_copy(out.at[:, span], out_hbm.at[:, span], out_sems.at[pair])
        send.start()
        sends.append(send)
    for send in sends:
        send.wait()


def backward(dy_recv, hidden, act, slope, weights):
    far = pl.BlockSpec(memory_space=pl.ANY)
    near = pl.BlockSpec(memory_space=pltpu.VMEM)
    back_shape = (Z, COLUMNS * PIECE, QWIDTH)
    return pl.pallas_call(
        backward_kernel,
        in_specs=[far] * 12 + [near] * 3,
        out_specs=[far, near],
        out_shape=[
            jax.ShapeDtypeStruct(back_shape, BF16),
            jax.ShapeDtypeStruct((Z, 128), F32),
        ],
        scratch_shapes=[
            pltpu.VMEM((COLUMNS, SLOTS, WIDTH), BF16),
            pltpu.VMEM((RECV, HID), BF16),
            pltpu.VMEM((RECV, HID), BF16),
            pltpu.VMEM((RECV, HID), BF16),
            pltpu.VMEM((WIDTH, 2 * HID), BF16),
            pltpu.VMEM((HID, WIDTH), BF16),
            pltpu.VMEM((RECV, 2 * HID), BF16),
            pltpu.VMEM((COLUMNS, QUARTERS, SLOTS, QWIDTH), BF16),
            pltpu.VMEM(back_shape, BF16),
            pltpu.SemaphoreType.DMA((17,)),
            pltpu.SemaphoreType.DMA((COLUMNS // 2,)),
        ],
        compiler_params=pltpu.CompilerParams(vmem_limit_bytes=56 * MIB),
        cost_estimate=pl.CostEstimate(
            flops=6 * RECV * WIDTH * HID, bytes_accessed=20000000, transcendentals=0
        ),
        name="backward",
    )(dy_recv, hidden, act, slope, *weights, turn_rows(), *term_tables())


def place_kernel(half_ref, ids_ref, gates_ref, spread_ref, wanted_ref, place_ref, code_ref):
    lane = lax.broadcasted_iota(jnp.int32, (TOK, EXPERTS), 1)
    core = (lane % 2).astype(F32)
    expert = lane - lane % 2 + half_ref[0]
    member = jnp.zeros((TOK, EXPERTS), F32)
    gate = jnp.zeros((TOK, EXPERTS), F32)
    for k in range(TOPK):
        same = ids_ref[:, k : k + 1] == expert
        value = gates_ref[:, k : k + 1].astype(F32) * (1.0 / 65536.0)
        member = member + jnp.where(same, 1.0, 0.0)
        gate = gate + jnp.where(same, value, 0.0)
    row = lax.broadcasted_iota(jnp.int32, (TOK, TOK), 0)
    column = lax.broadcasted_iota(jnp.int32, (TOK, TOK), 1)
    before = jnp.where(column < row, 1.0, 0.0).astype(BF16)
    rank = jnp.dot(before, member.astype(BF16), preferred_element_type=F32)
    upper = jnp.where(rank >= SHARE, 1.0, 0.0)
    code = jnp.where((member > 0.0) & (upper == core), rank - SHARE * upper, -1.0)
    code_ref[...] = code
    code_wide = jnp.dot(code.astype(BF16), spread_ref[...], preferred_element_type=F32)
    gate_wide = jnp.dot(gate.astype(BF16), spread_ref[...], preferred_element_type=F32)
    for q in range(QUARTERS):
        hit = code_wide == wanted_ref[q : q + 1, :]
        place_ref[q * TOK : (q + 1) * TOK, :] = jnp.where(hit, gate_wide, 0.0).astype(BF16)


def make_place(half, ids, gates):
    return pl.pallas_call(
        place_kernel,
        grid_spec=pltpu.PrefetchScalarGridSpec(
            num_scalar_prefetch=1,
            grid=(1,),
            in_specs=[
                whole((TOK, TOPK)),
                whole((TOK, TOPK)),
                whole((EXPERTS, BACK)),
                whole((8, BACK)),
            ],
            out_specs=[whole((QUARTERS * TOK, BACK)), whole((TOK, EXPERTS))],
        ),
        out_shape=[
            jax.ShapeDtypeStruct((QUARTERS * TOK, BACK), BF16),
            jax.ShapeDtypeStruct((TOK, EXPERTS), F32),
        ],
        compiler_params=pltpu.CompilerParams(vmem_limit_bytes=40 * MIB),
        cost_estimate=pl.CostEstimate(flops=300000000, bytes_accessed=4000000, transcendentals=0),
        name="place",
    )(half, ids, gates, *place_tables())


def terms_kernel(where_ref, code_ref, ids_ref, *refs):
    parts, (swapped_ref, mine_ref, theirs_ref, every, out) = refs[:5], refs[5:]
    half, core = where_ref[2], where_ref[3]

    def keep(distance, block):
        source = lax.rem(where_ref[1] + 2 * Z - distance, Z)
        every[pl.ds(pl.multiple_of(source * COLUMNS, COLUMNS), COLUMNS), :] = block

    keep(0, parts[0][...])
    keep(4, parts[4][...])
    for i in range(1, 4):
        keep(i + 4 * core, parts[i][...])
        keep(i + 4 * (1 - core), swapped_ref[(i - 1) * COLUMNS : i * COLUMNS, :])
    slot = lax.broadcasted_iota(jnp.int32, (8, 128), 0)
    lane = lax.broadcasted_iota(jnp.int32, (8, 128), 1)
    pick = jnp.where((lane == slot + where_ref[0]) & (slot < SHARE), 1.0, 0.0)
    term = lax.dot_general(
        pick.astype(BF16), every[...].astype(BF16), TURN, preferred_element_type=F32
    )
    found = jnp.zeros((TOK, EXPERTS), F32)
    for s in range(SHARE):
        found = found + jnp.where(code_ref[...] == float(s), term[s : s + 1, :], 0.0)
    column = lax.broadcasted_iota(jnp.int32, (TOK, EXPERTS), 1)
    expert = column - column % 2 + half
    total = jnp.zeros((TOK, 128), F32)
    for k in range(TOPK):
        hit = jnp.where(ids_ref[:, k : k + 1] == expert, found, 0.0)
        total = jnp.where(column == k, jnp.sum(hit, axis=1, keepdims=True), total)
    out[...] = total
    rows = TOK // 2
    mine_ref[...] = out[pl.ds(pl.multiple_of(half * rows, rows), rows), :]
    theirs_ref[...] = out[pl.ds(pl.multiple_of((1 - half) * rows, rows), rows), :]


def own_terms(where, parts, code, ids):
    near = pl.BlockSpec(memory_space=pltpu.VMEM)
    return pl.pallas_call(
        terms_kernel,
        in_specs=[pl.BlockSpec(memory_space=pltpu.SMEM)] + [near] * (2 + 6),
        out_specs=[near, near],
        out_shape=[jax.ShapeDtypeStruct((TOK // 2, 128), F32)] * 2,
        scratch_shapes=[pltpu.VMEM((EXPERTS, 128), F32), pltpu.VMEM((TOK, 128), F32)],
        cost_estimate=pl.CostEstimate(flops=1000000, bytes_accessed=300000, transcendentals=0),
        name="terms",
    )(where, code, ids, *parts)


def combine_kernel(
    half_ref, place_hbm, back_hbm, mine_ref, theirs_ref, place, back, total, sems
):
    depth = BACK // STEPS
    copies = []
    for i in range(STEPS):
        span = pl.ds(i * depth, depth)
        copies.append(
            (
                pltpu.make_async_copy(place_hbm.at[:, span], place.at[:, span], sems.at[2 * i]),
                pltpu.make_async_copy(back_hbm.at[span], back.at[span], sems.at[2 * i + 1]),
            )
        )
    for pair in copies:
        for copy in pair:
            copy.start()
    for i, pair in enumerate(copies):
        for copy in pair:
            copy.wait()
        span = slice(i * depth, (i + 1) * depth)
        part = jnp.dot(place[:, span], back[span, :], preferred_element_type=F32)
        total[...] = part if i == 0 else total[...] + part
    rows = TOK // 2
    for q in range(QUARTERS):
        span = slice(q * QWIDTH, (q + 1) * QWIDTH)
        own = pl.multiple_of(q * TOK + half_ref[0] * rows, rows)
        other = pl.multiple_of(q * TOK + (1 - half_ref[0]) * rows, rows)
        theirs_ref[:, span] = total[pl.ds(other, rows), :].astype(BF16)
        mine_ref[:, span] = total[pl.ds(own, rows), :]


STEPS = 4


def combine(half, place, back):
    near = pl.BlockSpec(memory_space=pltpu.VMEM)
    return pl.pallas_call(
        combine_kernel,
        in_specs=[
            pl.BlockSpec(memory_space=pltpu.SMEM),
            pl.BlockSpec(memory_space=pl.ANY),
            pl.BlockSpec(memory_space=pl.ANY),
        ],
        out_specs=[near, near],
        out_shape=[
            jax.ShapeDtypeStruct((TOK // 2, WIDTH), F32),
            jax.ShapeDtypeStruct((TOK // 2, WIDTH), BF16),
        ],
        scratch_shapes=[
            pltpu.VMEM((QUARTERS * TOK, BACK), BF16),
            pltpu.VMEM((BACK, QWIDTH), BF16),
            pltpu.VMEM((QUARTERS * TOK, QWIDTH), F32),
            pltpu.SemaphoreType.DMA((2 * STEPS,)),
        ],
        compiler_params=pltpu.CompilerParams(vmem_limit_bytes=56 * MIB),
        cost_estimate=pl.CostEstimate(
            flops=2 * QUARTERS * TOK * BACK * QWIDTH, bytes_accessed=8000000, transcendentals=0
        ),
        name="combine",
    )(half, place, back)


def finish_kernel(mine_ref, theirs_ref, router_ref, d_mine_ref, d_theirs_ref, grad_ref, d_gate_ref):
    total = mine_ref[...] + theirs_ref[...].astype(F32) + router_ref[...]
    grad_ref[...] = total.astype(BF16)
    d_gate_ref[...] = (d_mine_ref[...] + d_theirs_ref[...])[:, :TOPK]


def finish(mine, theirs, router_back, d_mine, d_theirs):
    near = pl.BlockSpec(memory_space=pltpu.VMEM)
    rows = TOK // 2
    return pl.pallas_call(
        finish_kernel,
        in_specs=[near] * 5,
        out_specs=[near, near],
        out_shape=[
            jax.ShapeDtypeStruct((rows, WIDTH), BF16),
            jax.ShapeDtypeStruct((rows, TOPK), F32),
        ],
        compiler_params=pltpu.CompilerParams(vmem_limit_bytes=16 * MIB),
        cost_estimate=pl.CostEstimate(flops=1000000, bytes_accessed=1500000, transcendentals=0),
        name="finish",
    )(mine, theirs, router_back, d_mine, d_theirs)


def on_device(tokens, grad_out, router_weight, expert_ids, gate_fixed, w_gate, w_up, w_down):
    z = lax.axis_index("z")
    yl = lax.axis_index("yl")
    c = lax.axis_index("c")
    column = (lax.axis_index("yh") * 4 + lax.axis_index("x")) * 2 + c
    at_home = c == yl
    half_index = yl.reshape(1).astype(jnp.int32)

    def cross(block):
        return lax.ppermute(block, ("c", "yl"), [(1, 2), (2, 1)])

    def other_core(block):
        return lax.ppermute(block, "c", [(0, 1), (1, 0)])

    def half_columns(block):
        return lax.dynamic_slice_in_dim(block, yl * HALF, HALF, 1)

    def exchange(block):
        return lax.all_to_all(block, PLANE, split_axis=0, concat_axis=0, tiled=True)

    def ring(block):
        ahead = [(i, (i + 1) % Z) for i in range(Z)]
        behind = [(i, (i - 1) % Z) for i in range(Z)]
        found, left, right = [block], block, block
        for step in range(4):
            if step == 3:
                left, right = left[: TOK // 2], right[TOK // 2 :]
            left, right = lax.ppermute(left, "z", ahead), lax.ppermute(right, "z", behind)
            found += [left, right]
        return found

    plane = z.reshape(1).astype(jnp.int32)
    cut = FF // 2
    blank = jnp.zeros((TOK, META - TOPK), BF16)
    x_meta = jnp.concatenate([half_columns(tokens), expert_ids.astype(BF16), blank], axis=1)
    x_meta, w_gate, w_up, w_down = lax.optimization_barrier(
        (x_meta, w_gate[0], w_up[0], w_down[0])
    )
    x_chunks = ring(x_meta)
    gate_c, up_c, down_c = cross(w_gate), cross(w_up), cross(w_down[:cut])
    dy_half, x_chunks[6] = lax.optimization_barrier((half_columns(grad_out), x_chunks[6]))
    dy_chunks = ring(dy_half)
    x_send, near_code, near_count = dispatch(plane, NEAR, x_chunks[:7])
    x_send, far_code, far_count = dispatch(plane, FAR, x_chunks[7:], before=x_send)
    counts = near_count + far_count
    x_send, gate_c, up_c, down_c, w_tail = lax.optimization_barrier(
        (x_send, gate_c, up_c, down_c, w_down[cut:])
    )
    tail_c = cross(w_tail)
    x_recv = exchange(x_send)
    gate_a = jnp.where(at_home, w_gate, gate_c)
    up_a = jnp.where(at_home, w_up, up_c)
    down_a = jnp.where(at_home, w_down[:cut], down_c)
    gate_b, up_b, down_b = other_core(gate_a), other_core(up_a), other_core(down_a)
    dy_send = dispatch(plane, NEAR, dy_chunks[:7], code=near_code)
    dy_send = dispatch(plane, FAR, dy_chunks[7:], before=dy_send, code=far_code)
    dy_send, tail_c = lax.optimization_barrier((dy_send, tail_c))
    dy_recv = exchange(dy_send)
    tail_a = jnp.where(at_home, w_tail, tail_c)
    tail_b = other_core(tail_a)
    hidden, act, slope = forward(
        x_recv.reshape(COLUMNS, 2, SLOTS, HALF), gate_a, gate_b, up_a, up_b
    )
    grads, terms = backward(
        dy_recv.reshape(COLUMNS, 2, SLOTS, HALF),
        hidden,
        act,
        slope,
        (gate_a, gate_b, up_a, up_b, down_a, down_b, tail_a, tail_b),
    )
    back = lax.all_to_all(
        grads.reshape(BACK, QWIDTH), SAME_SPLIT, split_axis=0, concat_axis=0, tiled=True
    )
    plane_news = lax.all_gather(
        jnp.concatenate([terms, counts], axis=0), ("yh", "x", "c"), axis=0, tiled=False
    )
    load = plane_news[:, Z].sum(axis=0)

    def terms_for(distance):
        return lax.dynamic_index_in_dim(plane_news, (z + distance) % Z, 1, keepdims=False)

    def turned_terms(step):
        route = []
        for i in range(Z):
            for core in range(2):
                distance = step + 4 * core if step < 4 else 4
                route.append((i * 2 + core, (i + distance) % Z * 2 + core))
        distance = step + 4 * c if step < 4 else 4
        return lax.ppermute(terms_for(distance), ("z", "c"), route)

    found_terms = [terms_for(0)] + [turned_terms(step) for step in range(1, 5)]

    half_rows = TOK // 2
    place, own_code = make_place(half_index, expert_ids, gate_fixed)
    swap = [(0, 1), (1, 0)]

    own_tokens = lax.dynamic_slice_in_dim(tokens, yl * half_rows, half_rows, 0)
    logits = jnp.dot(own_tokens, router_weight, preferred_element_type=F32)
    probs = jax.nn.softmax(logits, axis=1)
    share = load * EXPERTS / (EXPERTS * TOK * TOPK)
    d_logits = EXPERTS * probs * (
        share[None, :] - jnp.sum(probs * share[None, :], axis=1, keepdims=True)
    )
    router_back = lax.dot_general(
        d_logits.astype(BF16), router_weight, TURN, preferred_element_type=F32
    )

    back, router_back, place = lax.optimization_barrier((back, router_back, place))
    swapped = other_core(jnp.concatenate(found_terms[1:4], axis=0))
    mine, theirs = combine(half_index, place, back)
    theirs, swapped = lax.optimization_barrier((theirs, swapped))
    theirs = lax.ppermute(theirs, "yl", swap)
    where = jnp.stack([column * SHARE, z, yl, c]).astype(jnp.int32)
    d_mine, d_theirs = own_terms(where, [*found_terms, swapped], own_code, expert_ids)
    d_theirs = lax.ppermute(d_theirs, "yl", swap)
    grad_tokens, d_gate = finish(mine, theirs, router_back, d_mine, d_theirs)
    return grad_tokens, d_gate, d_logits


def solution(mesh):
    fine = Mesh(mesh.devices.reshape(8, 2, 4, 2, 2), ("z", "yh", "x", "c", "yl"))
    return jax.shard_map(
        on_device,
        mesh=fine,
        in_specs=(
            P(SAME_SPLIT, None),
            P(SAME_SPLIT, None),
            P(),
            P(SAME_SPLIT, None),
            P(SAME_SPLIT, None),
            P(SAME_SPLIT, None, "yl"),
            P(SAME_SPLIT, None, "yl"),
            P(SAME_SPLIT, "yl", None),
        ),
        out_specs=(
            P(SAME_SPLIT + ("yl",), None),
            P(SAME_SPLIT + ("yl",), None),
            P(SAME_SPLIT + ("yl",), None),
        ),
        check_vma=False,
    )
```

```python
import functools

import jax
import jax.numpy as jnp
import numpy as np
from jax import lax
from jax.experimental import pallas as pl
from jax.experimental.pallas import tpu as pltpu
from jax.sharding import Mesh
from jax.sharding import PartitionSpec as P

EXPERTS = 128
Z = 8
PLANE_EXPERTS = 16
COLUMNS = 16
TOK = 128
COL = Z * TOK
WIDTH = 2048
HALF = 1024
QUARTERS = 4
QWIDTH = WIDTH // QUARTERS
META = 128
SHARE = 6
SLOTS = Z * SHARE
GROUPS = 32
ROWS = GROUPS * SLOTS
RECV = COLUMNS * SLOTS
PIECE = QUARTERS * SHARE
BACK = EXPERTS * PIECE
FF = 384
HID = 2 * FF
TOPK = 8
F32 = jnp.float32
BF16 = jnp.bfloat16
PLANE = ("yh", "x", "c", "yl")
SAME_SPLIT = ("z", "yh", "x", "c")
TURN = (((1,), (1,)), ((), ()))
NEAR = (0, -1, 1, -2, 2, -3, 3)
FAR = (4,)
MIB = 1 << 20


def turn_rows():
    pair, quarter, source, slot = np.meshgrid(
        np.arange(2), np.arange(QUARTERS), np.arange(Z), np.arange(SHARE), indexing="ij"
    )
    have = (pair * QUARTERS + quarter) * SLOTS + source * SHARE + slot
    want = ((source * 2 + pair) * QUARTERS + quarter) * SHARE + slot
    table = np.zeros((2 * QUARTERS * SLOTS,) * 2, np.float32)
    table[want.reshape(-1), have.reshape(-1)] = 1.0
    return jnp.asarray(table, BF16)


def term_tables():
    row = np.arange(RECV)
    column, source, slot = row // SLOTS, row % SLOTS // SHARE, row % SHARE
    to_lane = np.zeros((RECV, 128), np.float32)
    to_lane[row, column * SHARE + slot] = 1.0
    to_source = np.zeros((Z, RECV), np.float32)
    to_source[source, row] = 1.0
    return jnp.asarray(to_source, BF16), jnp.asarray(to_lane, BF16)


def place_tables():
    lane = np.arange(BACK)
    spread = (np.arange(EXPERTS)[:, None] == lane[None, :] // PIECE).astype(np.float32)
    quarter, slot = lane % PIECE // SHARE, lane % SHARE
    wanted = np.where(quarter[None, :] == np.arange(8)[:, None], slot[None, :], -9.0)
    return jnp.asarray(spread, BF16), jnp.asarray(wanted, F32)


def whole(shape):
    return pl.BlockSpec(shape, lambda *_: (0,) * len(shape))


def slot_codes(plane, offsets, meta_refs, code_ref, count_ref, code_all):
    width = TOK * len(offsets)
    turned = jnp.concatenate([ref[...] for ref in meta_refs], axis=0).astype(F32).T
    expert = lax.broadcasted_iota(jnp.int32, (EXPERTS, width), 0).astype(F32)
    member = jnp.zeros((EXPERTS, width), F32)
    for k in range(TOPK):
        member = member + jnp.where(turned[k : k + 1, :] == expert, 1.0, 0.0)
    row = lax.broadcasted_iota(jnp.int32, (TOK, TOK), 0)
    column = lax.broadcasted_iota(jnp.int32, (TOK, TOK), 1)
    before = jnp.where(row < column, 1.0, 0.0).astype(BF16)
    low = member.astype(BF16)
    for i, offset in enumerate(offsets):
        source = lax.rem(plane + (offset + Z), Z)
        base = (source * SHARE).astype(F32)
        span = slice(i * TOK, (i + 1) * TOK)
        rank = jnp.dot(low[:, span], before, preferred_element_type=F32)
        code = rank + base + jnp.where(rank >= SHARE, float(SLOTS - SHARE), 0.0)
        code_all[:, span] = jnp.where(member[:, span] > 0.0, code, -1.0)
    first = pl.multiple_of(plane * PLANE_EXPERTS, PLANE_EXPERTS)
    code_ref[...] = code_all[pl.ds(first, PLANE_EXPERTS), :]
    count_ref[...] = lax.dot_general(
        jnp.ones((8, width), BF16), low, TURN, preferred_element_type=F32
    )


def gather_place(code_ref, place):
    slot = lax.broadcasted_iota(jnp.int32, (SLOTS, place.shape[1]), 0).astype(F32)
    for g in range(GROUPS):
        expert = (g // 4) * 2 + g % 2
        first = ((g // 2) % 2) * SLOTS
        hit = slot + float(first) == code_ref[expert : expert + 1, :]
        place[g * SLOTS : (g + 1) * SLOTS, :] = jnp.where(hit, 1.0, 0.0).astype(BF16)


def move_rows(chunk_refs, place, out_ref, before_ref=None):
    rows = jnp.concatenate([ref[...] for ref in chunk_refs], axis=0)
    part = jnp.dot(place[...], rows, preferred_element_type=F32)
    part = part.astype(BF16).reshape(out_ref.shape)
    out_ref[...] = part if before_ref is None else part + before_ref[...]


def route_kernel(offsets, count, more, plane_ref, *refs):
    metas, chunks, rest = refs[:count], refs[count : 2 * count], refs[2 * count :]
    before_ref = rest[0] if more else None
    out_ref, code_ref, count_ref, place, code_all = rest[more:]

    @pl.when(pl.program_id(0) == 0)
    def _():
        slot_codes(plane_ref[0], offsets, metas, code_ref, count_ref, code_all)
        gather_place(code_ref, place)

    move_rows(chunks, place, out_ref, before_ref)


def follow_kernel(count, more, plane_ref, code_ref, *refs):
    chunks, rest = refs[:count], refs[count:]
    before_ref = rest[0] if more else None
    out_ref, place = rest[more:]

    @pl.when(pl.program_id(0) == 0)
    def _():
        gather_place(code_ref, place)

    move_rows(chunks, place, out_ref, before_ref)


def dispatch(plane, offsets, chunks, before=None, code=None):
    block = 256
    count, more, width = len(chunks), int(before is not None), TOK * len(offsets)
    moved = pl.BlockSpec((GROUPS, SLOTS, block), lambda i, s: (0, 0, i))
    moved_shape = jax.ShapeDtypeStruct((GROUPS, SLOTS, HALF), BF16)
    meta_specs = [
        pl.BlockSpec((chunk.shape[0], META), lambda i, s: (0, HALF // META)) for chunk in chunks
    ]
    chunk_specs = [pl.BlockSpec((chunk.shape[0], block), lambda i, s: (0, i)) for chunk in chunks]
    tail = [before] if more else []
    place = pltpu.VMEM((ROWS, width), BF16)
    if code is None:
        kernel = functools.partial(route_kernel, offsets, count, more)
        operands = (*chunks, *chunks, *tail)
        in_specs = meta_specs + chunk_specs + [moved] * more
        out_specs = [moved, whole((PLANE_EXPERTS, width)), whole((8, EXPERTS))]
        out_shape = [
            moved_shape,
            jax.ShapeDtypeStruct((PLANE_EXPERTS, width), F32),
            jax.ShapeDtypeStruct((8, EXPERTS), F32),
        ]
        scratch = [place, pltpu.VMEM((EXPERTS, width), F32)]
    else:
        kernel = functools.partial(follow_kernel, count, more)
        operands = (code, *chunks, *tail)
        in_specs = [whole((PLANE_EXPERTS, width))] + chunk_specs + [moved] * more
        out_specs, out_shape, scratch = moved, moved_shape, [place]
    return pl.pallas_call(
        kernel,
        grid_spec=pltpu.PrefetchScalarGridSpec(
            num_scalar_prefetch=1,
            grid=(HALF // block,),
            in_specs=in_specs,
            out_specs=out_specs,
            scratch_shapes=scratch,
        ),
        out_shape=out_shape,
        compiler_params=pltpu.CompilerParams(vmem_limit_bytes=56 * MIB),
        cost_estimate=pl.CostEstimate(
            flops=2 * ROWS * width * HALF, bytes_accessed=5500000, transcendentals=0
        ),
        name="dispatch",
    )(plane, *operands)


def forward_kernel(x_ref, gate_a, gate_b, up_a, up_b, hidden_ref, act_ref, slope_ref):
    low = x_ref[:, 0].reshape(-1, HALF)
    high = x_ref[:, 1].reshape(-1, HALF)
    for i, (gate, up) in enumerate(((gate_a, up_a), (gate_b, up_b))):
        span = slice(i * FF, (i + 1) * FF)
        pre_gate = jnp.dot(low, gate[:HALF, :], preferred_element_type=F32) + jnp.dot(
            high, gate[HALF:, :], preferred_element_type=F32
        )
        pre_up = jnp.dot(low, up[:HALF, :], preferred_element_type=F32) + jnp.dot(
            high, up[HALF:, :], preferred_element_type=F32
        )
        sig = jax.nn.sigmoid(pre_gate)
        act = pre_gate * sig
        hidden_ref[:, span] = (act * pre_up).astype(BF16)
        act_ref[:, span] = act.astype(BF16)
        slope_ref[:, span] = (pre_up * sig * (1.0 + pre_gate * (1.0 - sig))).astype(BF16)


def forward(x_recv, gate_a, gate_b, up_a, up_b):
    steps = 2
    out = pl.BlockSpec((RECV // steps, HID), lambda i: (i, 0))
    return pl.pallas_call(
        forward_kernel,
        grid=(steps,),
        in_specs=[pl.BlockSpec((COLUMNS // steps, 2, SLOTS, HALF), lambda i: (i, 0, 0, 0))]
        + [whole((WIDTH, FF))] * 4,
        out_specs=[out] * 3,
        out_shape=[jax.ShapeDtypeStruct((RECV, HID), BF16)] * 3,
        compiler_params=pltpu.CompilerParams(vmem_limit_bytes=56 * MIB),
        cost_estimate=pl.CostEstimate(
            flops=4 * RECV * WIDTH * HID, bytes_accessed=14000000, transcendentals=RECV * HID
        ),
        name="forward",
    )(x_recv, gate_a, gate_b, up_a, up_b)


def backward_kernel(
    dy_hbm, hidden_hbm, act_hbm, slope_hbm, gate_a, gate_b, up_a, up_b, down_a, down_b, tail_a, tail_b,
    turn_ref, source_ref, lane_ref, out_ref, term_ref,
    dy, hidden, act, slope, ins, down, d_pre, grads, sems,
):
    cut = down_a.shape[0]
    copies = [
        pltpu.make_async_copy(dy_hbm.at[:, 0], dy.at[:, :, pl.ds(0, HALF)], sems.at[0]),
        pltpu.make_async_copy(dy_hbm.at[:, 1], dy.at[:, :, pl.ds(HALF, HALF)], sems.at[1]),
        pltpu.make_async_copy(down_a, down.at[pl.ds(0, cut)], sems.at[2]),
        pltpu.make_async_copy(down_b, down.at[pl.ds(FF, cut)], sems.at[3]),
        pltpu.make_async_copy(hidden_hbm, hidden, sems.at[4]),
        pltpu.make_async_copy(act_hbm, act, sems.at[5]),
        pltpu.make_async_copy(slope_hbm, slope, sems.at[6]),
    ]
    for i, weight in enumerate((gate_a, up_a, gate_b, up_b)):
        copies.append(
            pltpu.make_async_copy(weight, ins.at[:, pl.ds(i * FF, FF)], sems.at[7 + i])
        )
    tails = [
        pltpu.make_async_copy(tail_a, down.at[pl.ds(cut, FF - cut)], sems.at[11]),
        pltpu.make_async_copy(tail_b, down.at[pl.ds(FF + cut, FF - cut)], sems.at[12]),
    ]
    for copy in copies[:4] + tails + copies[4:]:
        copy.start()
    copies[0].wait()
    copies[1].wait()
    copies[2].wait()
    tails[0].wait()
    term = jnp.zeros((RECV, 1), F32)
    rows = dy[...].reshape(RECV, WIDTH)
    for i in range(2):
        span = slice(i * FF, (i + 1) * FF)
        if i == 1:
            copies[3].wait()
            tails[1].wait()
        d_hidden = lax.dot_general(rows, down[span, :], TURN, preferred_element_type=F32)
        if i == 0:
            copies[4].wait()
            copies[5].wait()
            copies[6].wait()
        term = term + jnp.sum(d_hidden * hidden[:, span].astype(F32), axis=1, keepdims=True)
        first = 2 * i * FF
        d_pre[:, first : first + FF] = (d_hidden * slope[:, span].astype(F32)).astype(BF16)
        d_pre[:, first + FF : first + 2 * FF] = (d_hidden * act[:, span].astype(F32)).astype(BF16)
    spread = jnp.where(lane_ref[...] > 0.0, term, 0.0).astype(BF16)
    term_ref[...] = jnp.dot(source_ref[...], spread, preferred_element_type=F32)
    for copy in copies[7:]:
        copy.wait()
    for q in range(QUARTERS):
        span = slice(q * QWIDTH, (q + 1) * QWIDTH)
        part = lax.dot_general(d_pre[...], ins[span, :], TURN, preferred_element_type=F32)
        grads[:, q] = part.astype(BF16).reshape(COLUMNS, SLOTS, QWIDTH)
    for pair in range(COLUMNS // 2):
        piece = grads[2 * pair : 2 * pair + 2].reshape(2 * QUARTERS * SLOTS, QWIDTH)
        moved = jnp.dot(turn_ref[...], piece, preferred_element_type=F32).astype(BF16)
        out_ref[:, pair * 2 * PIECE : (pair + 1) * 2 * PIECE, :] = moved.reshape(
            Z, 2 * PIECE, QWIDTH
        )


def backward(dy_recv, hidden, act, slope, weights):
    far = pl.BlockSpec(memory_space=pl.ANY)
    near = pl.BlockSpec(memory_space=pltpu.VMEM)
    back_shape = (Z, COLUMNS * PIECE, QWIDTH)
    return pl.pallas_call(
        backward_kernel,
        in_specs=[far] * 12 + [near] * 3,
        out_specs=[near, near],
        out_shape=[
            jax.ShapeDtypeStruct(back_shape, BF16),
            jax.ShapeDtypeStruct((Z, 128), F32),
        ],
        scratch_shapes=[
            pltpu.VMEM((COLUMNS, SLOTS, WIDTH), BF16),
            pltpu.VMEM((RECV, HID), BF16),
            pltpu.VMEM((RECV, HID), BF16),
            pltpu.VMEM((RECV, HID), BF16),
            pltpu.VMEM((WIDTH, 2 * HID), BF16),
            pltpu.VMEM((HID, WIDTH), BF16),
            pltpu.VMEM((RECV, 2 * HID), BF16),
            pltpu.VMEM((COLUMNS, QUARTERS, SLOTS, QWIDTH), BF16),
            pltpu.SemaphoreType.DMA((13,)),
        ],
        compiler_params=pltpu.CompilerParams(vmem_limit_bytes=56 * MIB),
        cost_estimate=pl.CostEstimate(
            flops=6 * RECV * WIDTH * HID, bytes_accessed=20000000, transcendentals=0
        ),
        name="backward",
    )(dy_recv, hidden, act, slope, *weights, turn_rows(), *term_tables())


def place_kernel(half_ref, ids_ref, gates_ref, spread_ref, wanted_ref, place_ref, code_ref):
    lane = lax.broadcasted_iota(jnp.int32, (TOK, EXPERTS), 1)
    core = (lane % 2).astype(F32)
    expert = lane - lane % 2 + half_ref[0]
    member = jnp.zeros((TOK, EXPERTS), F32)
    gate = jnp.zeros((TOK, EXPERTS), F32)
    for k in range(TOPK):
        same = ids_ref[:, k : k + 1] == expert
        value = gates_ref[:, k : k + 1].astype(F32) * (1.0 / 65536.0)
        member = member + jnp.where(same, 1.0, 0.0)
        gate = gate + jnp.where(same, value, 0.0)
    row = lax.broadcasted_iota(jnp.int32, (TOK, TOK), 0)
    column = lax.broadcasted_iota(jnp.int32, (TOK, TOK), 1)
    before = jnp.where(column < row, 1.0, 0.0).astype(BF16)
    rank = jnp.dot(before, member.astype(BF16), preferred_element_type=F32)
    upper = jnp.where(rank >= SHARE, 1.0, 0.0)
    code = jnp.where((member > 0.0) & (upper == core), rank - SHARE * upper, -1.0)
    code_ref[...] = code
    code_wide = jnp.dot(code.astype(BF16), spread_ref[...], preferred_element_type=F32)
    gate_wide = jnp.dot(gate.astype(BF16), spread_ref[...], preferred_element_type=F32)
    for q in range(QUARTERS):
        hit = code_wide == wanted_ref[q : q + 1, :]
        place_ref[q * TOK : (q + 1) * TOK, :] = jnp.where(hit, gate_wide, 0.0).astype(BF16)


def make_place(half, ids, gates):
    return pl.pallas_call(
        place_kernel,
        grid_spec=pltpu.PrefetchScalarGridSpec(
            num_scalar_prefetch=1,
            grid=(1,),
            in_specs=[
                whole((TOK, TOPK)),
                whole((TOK, TOPK)),
                whole((EXPERTS, BACK)),
                whole((8, BACK)),
            ],
            out_specs=[whole((QUARTERS * TOK, BACK)), whole((TOK, EXPERTS))],
        ),
        out_shape=[
            jax.ShapeDtypeStruct((QUARTERS * TOK, BACK), BF16),
            jax.ShapeDtypeStruct((TOK, EXPERTS), F32),
        ],
        compiler_params=pltpu.CompilerParams(vmem_limit_bytes=40 * MIB),
        cost_estimate=pl.CostEstimate(flops=300000000, bytes_accessed=4000000, transcendentals=0),
        name="place",
    )(half, ids, gates, *place_tables())


def terms_kernel(where_ref, code_ref, ids_ref, *refs):
    parts, (swapped_ref, mine_ref, theirs_ref, every, out) = refs[:5], refs[5:]
    half, core = where_ref[2], where_ref[3]

    def keep(distance, block):
        source = lax.rem(where_ref[1] + 2 * Z - distance, Z)
        every[pl.ds(pl.multiple_of(source * COLUMNS, COLUMNS), COLUMNS), :] = block

    keep(0, parts[0][...])
    keep(4, parts[4][...])
    for i in range(1, 4):
        keep(i + 4 * core, parts[i][...])
        keep(i + 4 * (1 - core), swapped_ref[(i - 1) * COLUMNS : i * COLUMNS, :])
    slot = lax.broadcasted_iota(jnp.int32, (8, 128), 0)
    lane = lax.broadcasted_iota(jnp.int32, (8, 128), 1)
    pick = jnp.where((lane == slot + where_ref[0]) & (slot < SHARE), 1.0, 0.0)
    term = lax.dot_general(
        pick.astype(BF16), every[...].astype(BF16), TURN, preferred_element_type=F32
    )
    found = jnp.zeros((TOK, EXPERTS), F32)
    for s in range(SHARE):
        found = found + jnp.where(code_ref[...] == float(s), term[s : s + 1, :], 0.0)
    column = lax.broadcasted_iota(jnp.int32, (TOK, EXPERTS), 1)
    expert = column - column % 2 + half
    total = jnp.zeros((TOK, 128), F32)
    for k in range(TOPK):
        hit = jnp.where(ids_ref[:, k : k + 1] == expert, found, 0.0)
        total = jnp.where(column == k, jnp.sum(hit, axis=1, keepdims=True), total)
    out[...] = total
    rows = TOK // 2
    mine_ref[...] = out[pl.ds(pl.multiple_of(half * rows, rows), rows), :]
    theirs_ref[...] = out[pl.ds(pl.multiple_of((1 - half) * rows, rows), rows), :]


def own_terms(where, parts, code, ids):
    near = pl.BlockSpec(memory_space=pltpu.VMEM)
    return pl.pallas_call(
        terms_kernel,
        in_specs=[pl.BlockSpec(memory_space=pltpu.SMEM)] + [near] * (2 + 6),
        out_specs=[near, near],
        out_shape=[jax.ShapeDtypeStruct((TOK // 2, 128), F32)] * 2,
        scratch_shapes=[pltpu.VMEM((EXPERTS, 128), F32), pltpu.VMEM((TOK, 128), F32)],
        cost_estimate=pl.CostEstimate(flops=1000000, bytes_accessed=300000, transcendentals=0),
        name="terms",
    )(where, code, ids, *parts)


def combine_kernel(
    half_ref, place_hbm, back_hbm, mine_ref, theirs_ref, place, back, total, sems
):
    depth = BACK // STEPS
    copies = []
    for i in range(STEPS):
        span = pl.ds(i * depth, depth)
        copies.append(
            (
                pltpu.make_async_copy(place_hbm.at[:, span], place.at[:, span], sems.at[2 * i]),
                pltpu.make_async_copy(back_hbm.at[span], back.at[span], sems.at[2 * i + 1]),
            )
        )
    for pair in copies:
        for copy in pair:
            copy.start()
    for i, pair in enumerate(copies):
        for copy in pair:
            copy.wait()
        span = slice(i * depth, (i + 1) * depth)
        part = jnp.dot(place[:, span], back[span, :], preferred_element_type=F32)
        total[...] = part if i == 0 else total[...] + part
    rows = TOK // 2
    for q in range(QUARTERS):
        span = slice(q * QWIDTH, (q + 1) * QWIDTH)
        own = pl.multiple_of(q * TOK + half_ref[0] * rows, rows)
        other = pl.multiple_of(q * TOK + (1 - half_ref[0]) * rows, rows)
        theirs_ref[:, span] = total[pl.ds(other, rows), :].astype(BF16)
        mine_ref[:, span] = total[pl.ds(own, rows), :]


STEPS = 4


def combine(half, place, back):
    near = pl.BlockSpec(memory_space=pltpu.VMEM)
    return pl.pallas_call(
        combine_kernel,
        in_specs=[
            pl.BlockSpec(memory_space=pltpu.SMEM),
            pl.BlockSpec(memory_space=pl.ANY),
            pl.BlockSpec(memory_space=pl.ANY),
        ],
        out_specs=[near, near],
        out_shape=[
            jax.ShapeDtypeStruct((TOK // 2, WIDTH), F32),
            jax.ShapeDtypeStruct((TOK // 2, WIDTH), BF16),
        ],
        scratch_shapes=[
            pltpu.VMEM((QUARTERS * TOK, BACK), BF16),
            pltpu.VMEM((BACK, QWIDTH), BF16),
            pltpu.VMEM((QUARTERS * TOK, QWIDTH), F32),
            pltpu.SemaphoreType.DMA((2 * STEPS,)),
        ],
        compiler_params=pltpu.CompilerParams(vmem_limit_bytes=56 * MIB),
        cost_estimate=pl.CostEstimate(
            flops=2 * QUARTERS * TOK * BACK * QWIDTH, bytes_accessed=8000000, transcendentals=0
        ),
        name="combine",
    )(half, place, back)


def finish_kernel(mine_ref, theirs_ref, router_ref, d_mine_ref, d_theirs_ref, grad_ref, d_gate_ref):
    total = mine_ref[...] + theirs_ref[...].astype(F32) + router_ref[...]
    grad_ref[...] = total.astype(BF16)
    d_gate_ref[...] = (d_mine_ref[...] + d_theirs_ref[...])[:, :TOPK]


def finish(mine, theirs, router_back, d_mine, d_theirs):
    near = pl.BlockSpec(memory_space=pltpu.VMEM)
    rows = TOK // 2
    return pl.pallas_call(
        finish_kernel,
        in_specs=[near] * 5,
        out_specs=[near, near],
        out_shape=[
            jax.ShapeDtypeStruct((rows, WIDTH), BF16),
            jax.ShapeDtypeStruct((rows, TOPK), F32),
        ],
        compiler_params=pltpu.CompilerParams(vmem_limit_bytes=16 * MIB),
        cost_estimate=pl.CostEstimate(flops=1000000, bytes_accessed=1500000, transcendentals=0),
        name="finish",
    )(mine, theirs, router_back, d_mine, d_theirs)


def on_device(tokens, grad_out, router_weight, expert_ids, gate_fixed, w_gate, w_up, w_down):
    z = lax.axis_index("z")
    yl = lax.axis_index("yl")
    c = lax.axis_index("c")
    column = (lax.axis_index("yh") * 4 + lax.axis_index("x")) * 2 + c
    at_home = c == yl
    half_index = yl.reshape(1).astype(jnp.int32)

    def cross(block):
        return lax.ppermute(block, ("c", "yl"), [(1, 2), (2, 1)])

    def other_core(block):
        return lax.ppermute(block, "c", [(0, 1), (1, 0)])

    def half_columns(block):
        return lax.dynamic_slice_in_dim(block, yl * HALF, HALF, 1)

    def exchange(block):
        return lax.all_to_all(block, PLANE, split_axis=0, concat_axis=0, tiled=True)

    def ring(block):
        ahead = [(i, (i + 1) % Z) for i in range(Z)]
        behind = [(i, (i - 1) % Z) for i in range(Z)]
        found, left, right = [block], block, block
        for step in range(4):
            if step == 3:
                left, right = left[: TOK // 2], right[TOK // 2 :]
            left, right = lax.ppermute(left, "z", ahead), lax.ppermute(right, "z", behind)
            found += [left, right]
        return found

    plane = z.reshape(1).astype(jnp.int32)
    cut = FF // 2
    blank = jnp.zeros((TOK, META - TOPK), BF16)
    x_meta = jnp.concatenate([half_columns(tokens), expert_ids.astype(BF16), blank], axis=1)
    w_gate, w_up, w_down = w_gate[0], w_up[0], w_down[0]
    x_chunks = ring(x_meta)
    gate_c, up_c, down_c = cross(w_gate), cross(w_up), cross(w_down[:cut])
    dy_half, x_chunks[6] = lax.optimization_barrier((half_columns(grad_out), x_chunks[6]))
    dy_chunks = ring(dy_half)
    x_send, near_code, near_count = dispatch(plane, NEAR, x_chunks[:7])
    x_send, far_code, far_count = dispatch(plane, FAR, x_chunks[7:], before=x_send)
    counts = near_count + far_count
    x_send, gate_c, up_c, down_c, w_tail = lax.optimization_barrier(
        (x_send, gate_c, up_c, down_c, w_down[cut:])
    )
    tail_c = cross(w_tail)
    x_recv = exchange(x_send)
    gate_a = jnp.where(at_home, w_gate, gate_c)
    up_a = jnp.where(at_home, w_up, up_c)
    down_a = jnp.where(at_home, w_down[:cut], down_c)
    gate_b, up_b, down_b = other_core(gate_a), other_core(up_a), other_core(down_a)
    dy_send = dispatch(plane, NEAR, dy_chunks[:7], code=near_code)
    dy_send = dispatch(plane, FAR, dy_chunks[7:], before=dy_send, code=far_code)
    dy_send, tail_c = lax.optimization_barrier((dy_send, tail_c))
    dy_recv = exchange(dy_send)
    tail_a = jnp.where(at_home, w_tail, tail_c)
    tail_b = other_core(tail_a)
    hidden, act, slope = forward(
        x_recv.reshape(COLUMNS, 2, SLOTS, HALF), gate_a, gate_b, up_a, up_b
    )
    grads, terms = backward(
        dy_recv.reshape(COLUMNS, 2, SLOTS, HALF),
        hidden,
        act,
        slope,
        (gate_a, gate_b, up_a, up_b, down_a, down_b, tail_a, tail_b),
    )
    back = lax.all_to_all(
        grads.reshape(BACK, QWIDTH), SAME_SPLIT, split_axis=0, concat_axis=0, tiled=True
    )
    plane_news = lax.all_gather(
        jnp.concatenate([terms, counts], axis=0), ("yh", "x", "c"), axis=0, tiled=False
    )
    load = plane_news[:, Z].sum(axis=0)

    def terms_for(distance):
        return lax.dynamic_index_in_dim(plane_news, (z + distance) % Z, 1, keepdims=False)

    def turned_terms(step):
        route = []
        for i in range(Z):
            for core in range(2):
                distance = step + 4 * core if step < 4 else 4
                route.append((i * 2 + core, (i + distance) % Z * 2 + core))
        distance = step + 4 * c if step < 4 else 4
        return lax.ppermute(terms_for(distance), ("z", "c"), route)

    found_terms = [terms_for(0)] + [turned_terms(step) for step in range(1, 5)]

    half_rows = TOK // 2
    place, own_code = make_place(half_index, expert_ids, gate_fixed)
    swap = [(0, 1), (1, 0)]

    own_tokens = lax.dynamic_slice_in_dim(tokens, yl * half_rows, half_rows, 0)
    logits = jnp.dot(own_tokens, router_weight, preferred_element_type=F32)
    probs = jax.nn.softmax(logits, axis=1)
    share = load * EXPERTS / (EXPERTS * TOK * TOPK)
    d_logits = EXPERTS * probs * (
        share[None, :] - jnp.sum(probs * share[None, :], axis=1, keepdims=True)
    )
    router_back = lax.dot_general(
        d_logits.astype(BF16), router_weight, TURN, preferred_element_type=F32
    )

    back, router_back, place, found_terms = lax.optimization_barrier(
        (back, router_back, place, found_terms)
    )
    swapped = other_core(jnp.concatenate(found_terms[1:4], axis=0))
    mine, theirs = combine(half_index, place, back)
    theirs, swapped = lax.optimization_barrier((theirs, swapped))
    theirs = lax.ppermute(theirs, "yl", swap)
    where = jnp.stack([column * SHARE, z, yl, c]).astype(jnp.int32)
    d_mine, d_theirs = own_terms(where, [*found_terms, swapped], own_code, expert_ids)
    d_theirs = lax.ppermute(d_theirs, "yl", swap)
    grad_tokens, d_gate = finish(mine, theirs, router_back, d_mine, d_theirs)
    return grad_tokens, d_gate, d_logits


def solution(mesh):
    fine = Mesh(mesh.devices.reshape(8, 2, 4, 2, 2), ("z", "yh", "x", "c", "yl"))
    return jax.shard_map(
        on_device,
        mesh=fine,
        in_specs=(
            P(SAME_SPLIT, None),
            P(SAME_SPLIT, None),
            P(),
            P(SAME_SPLIT, None),
            P(SAME_SPLIT, None),
            P(SAME_SPLIT, None, "yl"),
            P(SAME_SPLIT, None, "yl"),
            P(SAME_SPLIT, "yl", None),
        ),
        out_specs=(
            P(SAME_SPLIT + ("yl",), None),
            P(SAME_SPLIT + ("yl",), None),
            P(SAME_SPLIT + ("yl",), None),
        ),
        check_vma=False,
    )
```

```python
import jax
import jax.numpy as jnp
import numpy as np
from jax import lax
from jax.experimental import pallas as pl
from jax.experimental.pallas import tpu as pltpu
from jax.sharding import Mesh
from jax.sharding import PartitionSpec as P

EXPERTS = 128
Z = 8
PLANE_EXPERTS = 16
COLUMNS = 16
TOK = 128
COL = Z * TOK
WIDTH = 2048
HALF = 1024
QUARTERS = 4
QWIDTH = WIDTH // QUARTERS
META = 128
SHARE = 6
SLOTS = Z * SHARE
GROUPS = 32
ROWS = GROUPS * SLOTS
RECV = COLUMNS * SLOTS
PIECE = QUARTERS * SHARE
BACK = EXPERTS * PIECE
FF = 384
HID = 2 * FF
TOPK = 8
F32 = jnp.float32
BF16 = jnp.bfloat16
PLANE = ("yh", "x", "c", "yl")
SAME_SPLIT = ("z", "yh", "x", "c")
TURN = (((1,), (1,)), ((), ()))
OFFSETS = (0, -1, 1, -2, 2, -3, 3, 4)
MIB = 1 << 20


def turn_rows():
    pair, quarter, source, slot = np.meshgrid(
        np.arange(2), np.arange(QUARTERS), np.arange(Z), np.arange(SHARE), indexing="ij"
    )
    have = (pair * QUARTERS + quarter) * SLOTS + source * SHARE + slot
    want = ((source * 2 + pair) * QUARTERS + quarter) * SHARE + slot
    table = np.zeros((2 * QUARTERS * SLOTS,) * 2, np.float32)
    table[want.reshape(-1), have.reshape(-1)] = 1.0
    return jnp.asarray(table, BF16)


def term_tables():
    row = np.arange(RECV)
    column, source, slot = row // SLOTS, row % SLOTS // SHARE, row % SHARE
    to_lane = np.zeros((RECV, 128), np.float32)
    to_lane[row, column * SHARE + slot] = 1.0
    to_source = np.zeros((Z, RECV), np.float32)
    to_source[source, row] = 1.0
    return jnp.asarray(to_source, BF16), jnp.asarray(to_lane, BF16)


def place_tables():
    lane = np.arange(BACK)
    spread = (np.arange(EXPERTS)[:, None] == lane[None, :] // PIECE).astype(np.float32)
    quarter, slot = lane % PIECE // SHARE, lane % SHARE
    wanted = np.where(quarter[None, :] == np.arange(8)[:, None], slot[None, :], -9.0)
    return jnp.asarray(spread, BF16), jnp.asarray(wanted, F32)


def whole(shape):
    return pl.BlockSpec(shape, lambda *_: (0,) * len(shape))


def slot_codes(plane, meta_refs, code_ref, count_ref, code_all):
    turned = jnp.concatenate([ref[...] for ref in meta_refs], axis=0).astype(F32).T
    expert = lax.broadcasted_iota(jnp.int32, (EXPERTS, COL), 0).astype(F32)
    member = jnp.zeros((EXPERTS, COL), F32)
    for k in range(TOPK):
        member = member + jnp.where(turned[k : k + 1, :] == expert, 1.0, 0.0)
    row = lax.broadcasted_iota(jnp.int32, (TOK, TOK), 0)
    column = lax.broadcasted_iota(jnp.int32, (TOK, TOK), 1)
    before = jnp.where(row < column, 1.0, 0.0).astype(BF16)
    low = member.astype(BF16)
    for i, offset in enumerate(OFFSETS):
        source = lax.rem(plane + (offset + Z), Z)
        base = (source * SHARE).astype(F32)
        span = slice(i * TOK, (i + 1) * TOK)
        rank = jnp.dot(low[:, span], before, preferred_element_type=F32)
        code = rank + base + jnp.where(rank >= SHARE, float(SLOTS - SHARE), 0.0)
        code_all[:, span] = jnp.where(member[:, span] > 0.0, code, -1.0)
    first = pl.multiple_of(plane * PLANE_EXPERTS, PLANE_EXPERTS)
    code_ref[...] = code_all[pl.ds(first, PLANE_EXPERTS), :]
    count_ref[...] = lax.dot_general(
        jnp.ones((8, COL), BF16), low, TURN, preferred_element_type=F32
    )


def gather_place(code_ref, place):
    slot = lax.broadcasted_iota(jnp.int32, (SLOTS, COL), 0).astype(F32)
    for g in range(GROUPS):
        expert = (g // 4) * 2 + g % 2
        first = ((g // 2) % 2) * SLOTS
        hit = slot + float(first) == code_ref[expert : expert + 1, :]
        place[g * SLOTS : (g + 1) * SLOTS, :] = jnp.where(hit, 1.0, 0.0).astype(BF16)


def move_rows(chunk_refs, place, out_ref):
    rows = jnp.concatenate([ref[...] for ref in chunk_refs], axis=0)
    part = jnp.dot(place[...], rows, preferred_element_type=F32)
    out_ref[...] = part.astype(BF16).reshape(out_ref.shape)


def route_kernel(plane_ref, *refs):
    metas, chunks = refs[:Z], refs[Z : 2 * Z]
    out_ref, code_ref, count_ref, place, code_all = refs[2 * Z :]

    @pl.when(pl.program_id(0) == 0)
    def _():
        slot_codes(plane_ref[0], metas, code_ref, count_ref, code_all)
        gather_place(code_ref, place)

    move_rows(chunks, place, out_ref)


def follow_kernel(plane_ref, code_ref, *refs):
    chunks, (out_ref, place) = refs[:Z], refs[Z:]

    @pl.when(pl.program_id(0) == 0)
    def _():
        gather_place(code_ref, place)

    move_rows(chunks, place, out_ref)


def dispatch(plane, chunks, code=None):
    block = 256
    moved = pl.BlockSpec((GROUPS, SLOTS, block), lambda i, s: (0, 0, i))
    moved_shape = jax.ShapeDtypeStruct((GROUPS, SLOTS, HALF), BF16)
    chunk_specs = [pl.BlockSpec((TOK, block), lambda i, s: (0, i))] * Z
    place = pltpu.VMEM((ROWS, COL), BF16)
    if code is None:
        kernel = route_kernel
        operands = (*chunks, *chunks)
        in_specs = [pl.BlockSpec((TOK, META), lambda i, s: (0, HALF // META))] * Z + chunk_specs
        out_specs = [moved, whole((PLANE_EXPERTS, COL)), whole((8, EXPERTS))]
        out_shape = [
            moved_shape,
            jax.ShapeDtypeStruct((PLANE_EXPERTS, COL), F32),
            jax.ShapeDtypeStruct((8, EXPERTS), F32),
        ]
        scratch = [place, pltpu.VMEM((EXPERTS, COL), F32)]
    else:
        kernel = follow_kernel
        operands = (code, *chunks)
        in_specs = [whole((PLANE_EXPERTS, COL))] + chunk_specs
        out_specs, out_shape, scratch = moved, moved_shape, [place]
    return pl.pallas_call(
        kernel,
        grid_spec=pltpu.PrefetchScalarGridSpec(
            num_scalar_prefetch=1,
            grid=(HALF // block,),
            in_specs=in_specs,
            out_specs=out_specs,
            scratch_shapes=scratch,
        ),
        out_shape=out_shape,
        compiler_params=pltpu.CompilerParams(vmem_limit_bytes=56 * MIB),
        cost_estimate=pl.CostEstimate(
            flops=2 * ROWS * COL * HALF, bytes_accessed=5500000, transcendentals=0
        ),
        name="dispatch",
    )(plane, *operands)


def forward_kernel(x_ref, gate_a, gate_b, up_a, up_b, hidden_ref, act_ref, slope_ref):
    low = x_ref[:, 0].reshape(-1, HALF)
    high = x_ref[:, 1].reshape(-1, HALF)
    for i, (gate, up) in enumerate(((gate_a, up_a), (gate_b, up_b))):
        span = slice(i * FF, (i + 1) * FF)
        pre_gate = jnp.dot(low, gate[:HALF, :], preferred_element_type=F32) + jnp.dot(
            high, gate[HALF:, :], preferred_element_type=F32
        )
        pre_up = jnp.dot(low, up[:HALF, :], preferred_element_type=F32) + jnp.dot(
            high, up[HALF:, :], preferred_element_type=F32
        )
        sig = jax.nn.sigmoid(pre_gate)
        act = pre_gate * sig
        hidden_ref[:, span] = (act * pre_up).astype(BF16)
        act_ref[:, span] = act.astype(BF16)
        slope_ref[:, span] = (pre_up * sig * (1.0 + pre_gate * (1.0 - sig))).astype(BF16)


def forward(x_recv, gate_a, gate_b, up_a, up_b):
    steps = 2
    out = pl.BlockSpec((RECV // steps, HID), lambda i: (i, 0))
    return pl.pallas_call(
        forward_kernel,
        grid=(steps,),
        in_specs=[pl.BlockSpec((COLUMNS // steps, 2, SLOTS, HALF), lambda i: (i, 0, 0, 0))]
        + [whole((WIDTH, FF))] * 4,
        out_specs=[out] * 3,
        out_shape=[jax.ShapeDtypeStruct((RECV, HID), BF16)] * 3,
        compiler_params=pltpu.CompilerParams(vmem_limit_bytes=56 * MIB),
        cost_estimate=pl.CostEstimate(
            flops=4 * RECV * WIDTH * HID, bytes_accessed=14000000, transcendentals=RECV * HID
        ),
        name="forward",
    )(x_recv, gate_a, gate_b, up_a, up_b)


def backward_kernel(
    dy_hbm, hidden_hbm, act_hbm, slope_hbm, gate_a, gate_b, up_a, up_b, down_a, down_b, tail_a, tail_b,
    turn_ref, source_ref, lane_ref, out_ref, term_ref,
    dy, hidden, act, slope, ins, down, d_pre, grads, sems,
):
    cut = down_a.shape[0]
    copies = [
        pltpu.make_async_copy(dy_hbm.at[:, 0], dy.at[:, :, pl.ds(0, HALF)], sems.at[0]),
        pltpu.make_async_copy(dy_hbm.at[:, 1], dy.at[:, :, pl.ds(HALF, HALF)], sems.at[1]),
        pltpu.make_async_copy(down_a, down.at[pl.ds(0, cut)], sems.at[2]),
        pltpu.make_async_copy(down_b, down.at[pl.ds(FF, cut)], sems.at[3]),
        pltpu.make_async_copy(hidden_hbm, hidden, sems.at[4]),
        pltpu.make_async_copy(act_hbm, act, sems.at[5]),
        pltpu.make_async_copy(slope_hbm, slope, sems.at[6]),
    ]
    for i, weight in enumerate((gate_a, up_a, gate_b, up_b)):
        copies.append(
            pltpu.make_async_copy(weight, ins.at[:, pl.ds(i * FF, FF)], sems.at[7 + i])
        )
    tails = [
        pltpu.make_async_copy(tail_a, down.at[pl.ds(cut, FF - cut)], sems.at[11]),
        pltpu.make_async_copy(tail_b, down.at[pl.ds(FF + cut, FF - cut)], sems.at[12]),
    ]
    for copy in copies[:4] + tails + copies[4:]:
        copy.start()
    copies[0].wait()
    copies[1].wait()
    copies[2].wait()
    tails[0].wait()
    term = jnp.zeros((RECV, 1), F32)
    rows = dy[...].reshape(RECV, WIDTH)
    for i in range(2):
        span = slice(i * FF, (i + 1) * FF)
        if i == 1:
            copies[3].wait()
            tails[1].wait()
        d_hidden = lax.dot_general(rows, down[span, :], TURN, preferred_element_type=F32)
        if i == 0:
            copies[4].wait()
            copies[5].wait()
            copies[6].wait()
        term = term + jnp.sum(d_hidden * hidden[:, span].astype(F32), axis=1, keepdims=True)
        first = 2 * i * FF
        d_pre[:, first : first + FF] = (d_hidden * slope[:, span].astype(F32)).astype(BF16)
        d_pre[:, first + FF : first + 2 * FF] = (d_hidden * act[:, span].astype(F32)).astype(BF16)
    spread = jnp.where(lane_ref[...] > 0.0, term, 0.0).astype(BF16)
    term_ref[...] = jnp.dot(source_ref[...], spread, preferred_element_type=F32)
    for copy in copies[7:]:
        copy.wait()
    for q in range(QUARTERS):
        span = slice(q * QWIDTH, (q + 1) * QWIDTH)
        part = lax.dot_general(d_pre[...], ins[span, :], TURN, preferred_element_type=F32)
        grads[:, q] = part.astype(BF16).reshape(COLUMNS, SLOTS, QWIDTH)
    for pair in range(COLUMNS // 2):
        piece = grads[2 * pair : 2 * pair + 2].reshape(2 * QUARTERS * SLOTS, QWIDTH)
        moved = jnp.dot(turn_ref[...], piece, preferred_element_type=F32).astype(BF16)
        out_ref[:, pair * 2 * PIECE : (pair + 1) * 2 * PIECE, :] = moved.reshape(
            Z, 2 * PIECE, QWIDTH
        )


def backward(dy_recv, hidden, act, slope, weights):
    far = pl.BlockSpec(memory_space=pl.ANY)
    near = pl.BlockSpec(memory_space=pltpu.VMEM)
    back_shape = (Z, COLUMNS * PIECE, QWIDTH)
    return pl.pallas_call(
        backward_kernel,
        in_specs=[far] * 12 + [near] * 3,
        out_specs=[near, near],
        out_shape=[
            jax.ShapeDtypeStruct(back_shape, BF16),
            jax.ShapeDtypeStruct((Z, 128), F32),
        ],
        scratch_shapes=[
            pltpu.VMEM((COLUMNS, SLOTS, WIDTH), BF16),
            pltpu.VMEM((RECV, HID), BF16),
            pltpu.VMEM((RECV, HID), BF16),
            pltpu.VMEM((RECV, HID), BF16),
            pltpu.VMEM((WIDTH, 2 * HID), BF16),
            pltpu.VMEM((HID, WIDTH), BF16),
            pltpu.VMEM((RECV, 2 * HID), BF16),
            pltpu.VMEM((COLUMNS, QUARTERS, SLOTS, QWIDTH), BF16),
            pltpu.SemaphoreType.DMA((13,)),
        ],
        compiler_params=pltpu.CompilerParams(vmem_limit_bytes=56 * MIB),
        cost_estimate=pl.CostEstimate(
            flops=6 * RECV * WIDTH * HID, bytes_accessed=20000000, transcendentals=0
        ),
        name="backward",
    )(dy_recv, hidden, act, slope, *weights, turn_rows(), *term_tables())


def place_kernel(half_ref, ids_ref, gates_ref, spread_ref, wanted_ref, place_ref, code_ref):
    lane = lax.broadcasted_iota(jnp.int32, (TOK, EXPERTS), 1)
    core = (lane % 2).astype(F32)
    expert = lane - lane % 2 + half_ref[0]
    member = jnp.zeros((TOK, EXPERTS), F32)
    gate = jnp.zeros((TOK, EXPERTS), F32)
    for k in range(TOPK):
        same = ids_ref[:, k : k + 1] == expert
        value = gates_ref[:, k : k + 1].astype(F32) * (1.0 / 65536.0)
        member = member + jnp.where(same, 1.0, 0.0)
        gate = gate + jnp.where(same, value, 0.0)
    row = lax.broadcasted_iota(jnp.int32, (TOK, TOK), 0)
    column = lax.broadcasted_iota(jnp.int32, (TOK, TOK), 1)
    before = jnp.where(column < row, 1.0, 0.0).astype(BF16)
    rank = jnp.dot(before, member.astype(BF16), preferred_element_type=F32)
    upper = jnp.where(rank >= SHARE, 1.0, 0.0)
    code = jnp.where((member > 0.0) & (upper == core), rank - SHARE * upper, -1.0)
    code_ref[...] = code
    code_wide = jnp.dot(code.astype(BF16), spread_ref[...], preferred_element_type=F32)
    gate_wide = jnp.dot(gate.astype(BF16), spread_ref[...], preferred_element_type=F32)
    for q in range(QUARTERS):
        hit = code_wide == wanted_ref[q : q + 1, :]
        place_ref[q * TOK : (q + 1) * TOK, :] = jnp.where(hit, gate_wide, 0.0).astype(BF16)


def make_place(half, ids, gates):
    return pl.pallas_call(
        place_kernel,
        grid_spec=pltpu.PrefetchScalarGridSpec(
            num_scalar_prefetch=1,
            grid=(1,),
            in_specs=[
                whole((TOK, TOPK)),
                whole((TOK, TOPK)),
                whole((EXPERTS, BACK)),
                whole((8, BACK)),
            ],
            out_specs=[whole((QUARTERS * TOK, BACK)), whole((TOK, EXPERTS))],
        ),
        out_shape=[
            jax.ShapeDtypeStruct((QUARTERS * TOK, BACK), BF16),
            jax.ShapeDtypeStruct((TOK, EXPERTS), F32),
        ],
        compiler_params=pltpu.CompilerParams(vmem_limit_bytes=40 * MIB),
        cost_estimate=pl.CostEstimate(flops=300000000, bytes_accessed=4000000, transcendentals=0),
        name="place",
    )(half, ids, gates, *place_tables())


def terms_kernel(where_ref, code_ref, ids_ref, *refs):
    parts, (swapped_ref, mine_ref, theirs_ref, every, out) = refs[:5], refs[5:]
    half, core = where_ref[2], where_ref[3]

    def keep(distance, block):
        source = lax.rem(where_ref[1] + 2 * Z - distance, Z)
        every[pl.ds(pl.multiple_of(source * COLUMNS, COLUMNS), COLUMNS), :] = block

    keep(0, parts[0][...])
    keep(4, parts[4][...])
    for i in range(1, 4):
        keep(i + 4 * core, parts[i][...])
        keep(i + 4 * (1 - core), swapped_ref[(i - 1) * COLUMNS : i * COLUMNS, :])
    slot = lax.broadcasted_iota(jnp.int32, (8, 128), 0)
    lane = lax.broadcasted_iota(jnp.int32, (8, 128), 1)
    pick = jnp.where((lane == slot + where_ref[0]) & (slot < SHARE), 1.0, 0.0)
    term = lax.dot_general(
        pick.astype(BF16), every[...].astype(BF16), TURN, preferred_element_type=F32
    )
    found = jnp.zeros((TOK, EXPERTS), F32)
    for s in range(SHARE):
        found = found + jnp.where(code_ref[...] == float(s), term[s : s + 1, :], 0.0)
    column = lax.broadcasted_iota(jnp.int32, (TOK, EXPERTS), 1)
    expert = column - column % 2 + half
    total = jnp.zeros((TOK, 128), F32)
    for k in range(TOPK):
        hit = jnp.where(ids_ref[:, k : k + 1] == expert, found, 0.0)
        total = jnp.where(column == k, jnp.sum(hit, axis=1, keepdims=True), total)
    out[...] = total
    rows = TOK // 2
    mine_ref[...] = out[pl.ds(pl.multiple_of(half * rows, rows), rows), :]
    theirs_ref[...] = out[pl.ds(pl.multiple_of((1 - half) * rows, rows), rows), :]


def own_terms(where, parts, code, ids):
    near = pl.BlockSpec(memory_space=pltpu.VMEM)
    return pl.pallas_call(
        terms_kernel,
        in_specs=[pl.BlockSpec(memory_space=pltpu.SMEM)] + [near] * (2 + 6),
        out_specs=[near, near],
        out_shape=[jax.ShapeDtypeStruct((TOK // 2, 128), F32)] * 2,
        scratch_shapes=[pltpu.VMEM((EXPERTS, 128), F32), pltpu.VMEM((TOK, 128), F32)],
        cost_estimate=pl.CostEstimate(flops=1000000, bytes_accessed=300000, transcendentals=0),
        name="terms",
    )(where, code, ids, *parts)


def combine_kernel(
    half_ref, place_hbm, back_hbm, mine_ref, theirs_ref, place, back, total, sems
):
    depth = BACK // STEPS
    copies = []
    for i in range(STEPS):
        span = pl.ds(i * depth, depth)
        copies.append(
            (
                pltpu.make_async_copy(place_hbm.at[:, span], place.at[:, span], sems.at[2 * i]),
                pltpu.make_async_copy(back_hbm.at[span], back.at[span], sems.at[2 * i + 1]),
            )
        )
    for pair in copies:
        for copy in pair:
            copy.start()
    for i, pair in enumerate(copies):
        for copy in pair:
            copy.wait()
        span = slice(i * depth, (i + 1) * depth)
        part = jnp.dot(place[:, span], back[span, :], preferred_element_type=F32)
        total[...] = part if i == 0 else total[...] + part
    rows = TOK // 2
    for q in range(QUARTERS):
        span = slice(q * QWIDTH, (q + 1) * QWIDTH)
        own = pl.multiple_of(q * TOK + half_ref[0] * rows, rows)
        other = pl.multiple_of(q * TOK + (1 - half_ref[0]) * rows, rows)
        theirs_ref[:, span] = total[pl.ds(other, rows), :].astype(BF16)
        mine_ref[:, span] = total[pl.ds(own, rows), :]


STEPS = 4


def combine(half, place, back):
    near = pl.BlockSpec(memory_space=pltpu.VMEM)
    return pl.pallas_call(
        combine_kernel,
        in_specs=[
            pl.BlockSpec(memory_space=pltpu.SMEM),
            pl.BlockSpec(memory_space=pl.ANY),
            pl.BlockSpec(memory_space=pl.ANY),
        ],
        out_specs=[near, near],
        out_shape=[
            jax.ShapeDtypeStruct((TOK // 2, WIDTH), F32),
            jax.ShapeDtypeStruct((TOK // 2, WIDTH), BF16),
        ],
        scratch_shapes=[
            pltpu.VMEM((QUARTERS * TOK, BACK), BF16),
            pltpu.VMEM((BACK, QWIDTH), BF16),
            pltpu.VMEM((QUARTERS * TOK, QWIDTH), F32),
            pltpu.SemaphoreType.DMA((2 * STEPS,)),
        ],
        compiler_params=pltpu.CompilerParams(vmem_limit_bytes=56 * MIB),
        cost_estimate=pl.CostEstimate(
            flops=2 * QUARTERS * TOK * BACK * QWIDTH, bytes_accessed=8000000, transcendentals=0
        ),
        name="combine",
    )(half, place, back)


def finish_kernel(mine_ref, theirs_ref, router_ref, d_mine_ref, d_theirs_ref, grad_ref, d_gate_ref):
    total = mine_ref[...] + theirs_ref[...].astype(F32) + router_ref[...]
    grad_ref[...] = total.astype(BF16)
    d_gate_ref[...] = (d_mine_ref[...] + d_theirs_ref[...])[:, :TOPK]


def finish(mine, theirs, router_back, d_mine, d_theirs):
    near = pl.BlockSpec(memory_space=pltpu.VMEM)
    rows = TOK // 2
    return pl.pallas_call(
        finish_kernel,
        in_specs=[near] * 5,
        out_specs=[near, near],
        out_shape=[
            jax.ShapeDtypeStruct((rows, WIDTH), BF16),
            jax.ShapeDtypeStruct((rows, TOPK), F32),
        ],
        compiler_params=pltpu.CompilerParams(vmem_limit_bytes=16 * MIB),
        cost_estimate=pl.CostEstimate(flops=1000000, bytes_accessed=1500000, transcendentals=0),
        name="finish",
    )(mine, theirs, router_back, d_mine, d_theirs)


def on_device(tokens, grad_out, router_weight, expert_ids, gate_fixed, w_gate, w_up, w_down):
    z = lax.axis_index("z")
    yl = lax.axis_index("yl")
    c = lax.axis_index("c")
    column = (lax.axis_index("yh") * 4 + lax.axis_index("x")) * 2 + c
    at_home = c == yl
    half_index = yl.reshape(1).astype(jnp.int32)

    def cross(block):
        return lax.ppermute(block, ("c", "yl"), [(1, 2), (2, 1)])

    def other_core(block):
        return lax.ppermute(block, "c", [(0, 1), (1, 0)])

    def half_columns(block):
        return lax.dynamic_slice_in_dim(block, yl * HALF, HALF, 1)

    def exchange(block):
        return lax.all_to_all(block, PLANE, split_axis=0, concat_axis=0, tiled=True)

    def ring(block):
        ahead = [(i, (i + 1) % Z) for i in range(Z)]
        behind = [(i, (i - 1) % Z) for i in range(Z)]
        found, left, right = [block], block, block
        for _ in range(3):
            left, right = lax.ppermute(left, "z", ahead), lax.ppermute(right, "z", behind)
            found += [left, right]
        both = [(2 * i, 2 * j) for i, j in ahead] + [(2 * i + 1, 2 * j + 1) for i, j in behind]
        return [*found, lax.ppermute(jnp.where(c == 0, left, right), ("z", "c"), both)]

    plane = z.reshape(1).astype(jnp.int32)
    cut = FF // 2
    blank = jnp.zeros((TOK, META - TOPK), BF16)
    x_meta = jnp.concatenate([half_columns(tokens), expert_ids.astype(BF16), blank], axis=1)
    w_gate, w_up, w_down = w_gate[0], w_up[0], w_down[0]
    x_chunks = ring(x_meta)
    gate_c, up_c, down_c = cross(w_gate), cross(w_up), cross(w_down[:cut])
    dy_half, x_chunks[6] = lax.optimization_barrier((half_columns(grad_out), x_chunks[6]))
    dy_chunks = ring(dy_half)
    x_send, code, counts = dispatch(plane, x_chunks)
    x_send, gate_c, up_c, down_c, w_tail = lax.optimization_barrier(
        (x_send, gate_c, up_c, down_c, w_down[cut:])
    )
    tail_c = cross(w_tail)
    x_recv = exchange(x_send)
    gate_a = jnp.where(at_home, w_gate, gate_c)
    up_a = jnp.where(at_home, w_up, up_c)
    down_a = jnp.where(at_home, w_down[:cut], down_c)
    gate_b, up_b, down_b = other_core(gate_a), other_core(up_a), other_core(down_a)
    dy_send = dispatch(plane, dy_chunks, code=code)
    dy_send, tail_c = lax.optimization_barrier((dy_send, tail_c))
    dy_recv = exchange(dy_send)
    tail_a = jnp.where(at_home, w_tail, tail_c)
    tail_b = other_core(tail_a)
    hidden, act, slope = forward(
        x_recv.reshape(COLUMNS, 2, SLOTS, HALF), gate_a, gate_b, up_a, up_b
    )
    grads, terms = backward(
        dy_recv.reshape(COLUMNS, 2, SLOTS, HALF),
        hidden,
        act,
        slope,
        (gate_a, gate_b, up_a, up_b, down_a, down_b, tail_a, tail_b),
    )
    back = lax.all_to_all(
        grads.reshape(BACK, QWIDTH), SAME_SPLIT, split_axis=0, concat_axis=0, tiled=True
    )
    plane_news = lax.all_gather(
        jnp.concatenate([terms, counts], axis=0), ("yh", "x", "c"), axis=0, tiled=False
    )
    load = plane_news[:, Z].sum(axis=0)

    def terms_for(distance):
        return lax.dynamic_index_in_dim(plane_news, (z + distance) % Z, 1, keepdims=False)

    def turned_terms(step):
        route = []
        for i in range(Z):
            for core in range(2):
                distance = step + 4 * core if step < 4 else 4
                route.append((i * 2 + core, (i + distance) % Z * 2 + core))
        distance = step + 4 * c if step < 4 else 4
        return lax.ppermute(terms_for(distance), ("z", "c"), route)

    found_terms = [terms_for(0)] + [turned_terms(step) for step in range(1, 5)]

    half_rows = TOK // 2
    place, own_code = make_place(half_index, expert_ids, gate_fixed)
    swap = [(0, 1), (1, 0)]

    own_tokens = lax.dynamic_slice_in_dim(tokens, yl * half_rows, half_rows, 0)
    logits = jnp.dot(own_tokens, router_weight, preferred_element_type=F32)
    probs = jax.nn.softmax(logits, axis=1)
    share = load * EXPERTS / (EXPERTS * TOK * TOPK)
    d_logits = EXPERTS * probs * (
        share[None, :] - jnp.sum(probs * share[None, :], axis=1, keepdims=True)
    )
    router_back = lax.dot_general(
        d_logits.astype(BF16), router_weight, TURN, preferred_element_type=F32
    )

    back, router_back, place, found_terms = lax.optimization_barrier(
        (back, router_back, place, found_terms)
    )
    swapped = other_core(jnp.concatenate(found_terms[1:4], axis=0))
    mine, theirs = combine(half_index, place, back)
    theirs, swapped = lax.optimization_barrier((theirs, swapped))
    theirs = lax.ppermute(theirs, "yl", swap)
    where = jnp.stack([column * SHARE, z, yl, c]).astype(jnp.int32)
    d_mine, d_theirs = own_terms(where, [*found_terms, swapped], own_code, expert_ids)
    d_theirs = lax.ppermute(d_theirs, "yl", swap)
    grad_tokens, d_gate = finish(mine, theirs, router_back, d_mine, d_theirs)
    return grad_tokens, d_gate, d_logits


def solution(mesh):
    fine = Mesh(mesh.devices.reshape(8, 2, 4, 2, 2), ("z", "yh", "x", "c", "yl"))
    return jax.shard_map(
        on_device,
        mesh=fine,
        in_specs=(
            P(SAME_SPLIT, None),
            P(SAME_SPLIT, None),
            P(),
            P(SAME_SPLIT, None),
            P(SAME_SPLIT, None),
            P(SAME_SPLIT, None, "yl"),
            P(SAME_SPLIT, None, "yl"),
            P(SAME_SPLIT, "yl", None),
        ),
        out_specs=(
            P(SAME_SPLIT + ("yl",), None),
            P(SAME_SPLIT + ("yl",), None),
            P(SAME_SPLIT + ("yl",), None),
        ),
        check_vma=False,
    )
```

```python
import jax
import jax.numpy as jnp
import numpy as np
from jax import lax
from jax.experimental import pallas as pl
from jax.experimental.pallas import tpu as pltpu
from jax.sharding import Mesh
from jax.sharding import PartitionSpec as P

EXPERTS = 128
Z = 8
PLANE_EXPERTS = 16
COLUMNS = 16
TOK = 128
COL = Z * TOK
WIDTH = 2048
HALF = 1024
QUARTERS = 4
QWIDTH = WIDTH // QUARTERS
META = 128
SHARE = 6
SLOTS = Z * SHARE
GROUPS = 32
ROWS = GROUPS * SLOTS
RECV = COLUMNS * SLOTS
PIECE = QUARTERS * SHARE
BACK = EXPERTS * PIECE
FF = 384
HID = 2 * FF
TOPK = 8
F32 = jnp.float32
BF16 = jnp.bfloat16
PLANE = ("yh", "x", "c", "yl")
SAME_SPLIT = ("z", "yh", "x", "c")
TURN = (((1,), (1,)), ((), ()))
OFFSETS = (0, -1, 1, -2, 2, -3, 3, 4)
MIB = 1 << 20


def turn_rows():
    pair, quarter, source, slot = np.meshgrid(
        np.arange(2), np.arange(QUARTERS), np.arange(Z), np.arange(SHARE), indexing="ij"
    )
    have = (pair * QUARTERS + quarter) * SLOTS + source * SHARE + slot
    want = ((source * 2 + pair) * QUARTERS + quarter) * SHARE + slot
    table = np.zeros((2 * QUARTERS * SLOTS,) * 2, np.float32)
    table[want.reshape(-1), have.reshape(-1)] = 1.0
    return jnp.asarray(table, BF16)


def term_tables():
    row = np.arange(RECV)
    column, source, slot = row // SLOTS, row % SLOTS // SHARE, row % SHARE
    to_lane = np.zeros((RECV, 128), np.float32)
    to_lane[row, column * SHARE + slot] = 1.0
    to_source = np.zeros((Z, RECV), np.float32)
    to_source[source, row] = 1.0
    return jnp.asarray(to_source, BF16), jnp.asarray(to_lane, BF16)


def place_tables():
    lane = np.arange(BACK)
    spread = (np.arange(EXPERTS)[:, None] == lane[None, :] // PIECE).astype(np.float32)
    quarter, slot = lane % PIECE // SHARE, lane % SHARE
    wanted = np.where(quarter[None, :] == np.arange(8)[:, None], slot[None, :], -9.0)
    return jnp.asarray(spread, BF16), jnp.asarray(wanted, F32)


def whole(shape):
    return pl.BlockSpec(shape, lambda *_: (0,) * len(shape))


def slot_codes(plane, meta_refs, code_ref, count_ref, code_all):
    turned = jnp.concatenate([ref[...] for ref in meta_refs], axis=0).astype(F32).T
    expert = lax.broadcasted_iota(jnp.int32, (EXPERTS, COL), 0).astype(F32)
    member = jnp.zeros((EXPERTS, COL), F32)
    for k in range(TOPK):
        member = member + jnp.where(turned[k : k + 1, :] == expert, 1.0, 0.0)
    row = lax.broadcasted_iota(jnp.int32, (TOK, TOK), 0)
    column = lax.broadcasted_iota(jnp.int32, (TOK, TOK), 1)
    before = jnp.where(row < column, 1.0, 0.0).astype(BF16)
    low = member.astype(BF16)
    for i, offset in enumerate(OFFSETS):
        source = lax.rem(plane + (offset + Z), Z)
        base = (source * SHARE).astype(F32)
        span = slice(i * TOK, (i + 1) * TOK)
        rank = jnp.dot(low[:, span], before, preferred_element_type=F32)
        code = rank + base + jnp.where(rank >= SHARE, float(SLOTS - SHARE), 0.0)
        code_all[:, span] = jnp.where(member[:, span] > 0.0, code, -1.0)
    first = pl.multiple_of(plane * PLANE_EXPERTS, PLANE_EXPERTS)
    code_ref[...] = code_all[pl.ds(first, PLANE_EXPERTS), :]
    count_ref[...] = lax.dot_general(
        jnp.ones((8, COL), BF16), low, TURN, preferred_element_type=F32
    )


def gather_place(code_ref, place):
    slot = lax.broadcasted_iota(jnp.int32, (SLOTS, COL), 0).astype(F32)
    for g in range(GROUPS):
        expert = (g // 4) * 2 + g % 2
        first = ((g // 2) % 2) * SLOTS
        hit = slot + float(first) == code_ref[expert : expert + 1, :]
        place[g * SLOTS : (g + 1) * SLOTS, :] = jnp.where(hit, 1.0, 0.0).astype(BF16)


def move_rows(chunk_refs, place, out_ref):
    rows = jnp.concatenate([ref[...] for ref in chunk_refs], axis=0)
    part = jnp.dot(place[...], rows, preferred_element_type=F32)
    out_ref[...] = part.astype(BF16).reshape(out_ref.shape)


def route_kernel(plane_ref, *refs):
    metas, chunks = refs[:Z], refs[Z : 2 * Z]
    out_ref, code_ref, count_ref, place, code_all = refs[2 * Z :]

    @pl.when(pl.program_id(0) == 0)
    def _():
        slot_codes(plane_ref[0], metas, code_ref, count_ref, code_all)
        gather_place(code_ref, place)

    move_rows(chunks, place, out_ref)


def follow_kernel(plane_ref, code_ref, *refs):
    chunks, (out_ref, place) = refs[:Z], refs[Z:]

    @pl.when(pl.program_id(0) == 0)
    def _():
        gather_place(code_ref, place)

    move_rows(chunks, place, out_ref)


def dispatch(plane, chunks, code=None):
    block = 256
    moved = pl.BlockSpec((GROUPS, SLOTS, block), lambda i, s: (0, 0, i))
    moved_shape = jax.ShapeDtypeStruct((GROUPS, SLOTS, HALF), BF16)
    chunk_specs = [pl.BlockSpec((TOK, block), lambda i, s: (0, i))] * Z
    place = pltpu.VMEM((ROWS, COL), BF16)
    if code is None:
        kernel = route_kernel
        operands = (*chunks, *chunks)
        in_specs = [pl.BlockSpec((TOK, META), lambda i, s: (0, HALF // META))] * Z + chunk_specs
        out_specs = [moved, whole((PLANE_EXPERTS, COL)), whole((8, EXPERTS))]
        out_shape = [
            moved_shape,
            jax.ShapeDtypeStruct((PLANE_EXPERTS, COL), F32),
            jax.ShapeDtypeStruct((8, EXPERTS), F32),
        ]
        scratch = [place, pltpu.VMEM((EXPERTS, COL), F32)]
    else:
        kernel = follow_kernel
        operands = (code, *chunks)
        in_specs = [whole((PLANE_EXPERTS, COL))] + chunk_specs
        out_specs, out_shape, scratch = moved, moved_shape, [place]
    return pl.pallas_call(
        kernel,
        grid_spec=pltpu.PrefetchScalarGridSpec(
            num_scalar_prefetch=1,
            grid=(HALF // block,),
            in_specs=in_specs,
            out_specs=out_specs,
            scratch_shapes=scratch,
        ),
        out_shape=out_shape,
        compiler_params=pltpu.CompilerParams(vmem_limit_bytes=56 * MIB),
        cost_estimate=pl.CostEstimate(
            flops=2 * ROWS * COL * HALF, bytes_accessed=5500000, transcendentals=0
        ),
        name="dispatch",
    )(plane, *operands)


def forward_kernel(x_ref, gate_a, gate_b, up_a, up_b, hidden_ref, act_ref, slope_ref):
    low = x_ref[:, 0].reshape(-1, HALF)
    high = x_ref[:, 1].reshape(-1, HALF)
    for i, (gate, up) in enumerate(((gate_a, up_a), (gate_b, up_b))):
        span = slice(i * FF, (i + 1) * FF)
        pre_gate = jnp.dot(low, gate[:HALF, :], preferred_element_type=F32) + jnp.dot(
            high, gate[HALF:, :], preferred_element_type=F32
        )
        pre_up = jnp.dot(low, up[:HALF, :], preferred_element_type=F32) + jnp.dot(
            high, up[HALF:, :], preferred_element_type=F32
        )
        sig = jax.nn.sigmoid(pre_gate)
        act = pre_gate * sig
        hidden_ref[:, span] = (act * pre_up).astype(BF16)
        act_ref[:, span] = act.astype(BF16)
        slope_ref[:, span] = (pre_up * sig * (1.0 + pre_gate * (1.0 - sig))).astype(BF16)


def forward(x_recv, gate_a, gate_b, up_a, up_b):
    steps = 2
    out = pl.BlockSpec((RECV // steps, HID), lambda i: (i, 0))
    return pl.pallas_call(
        forward_kernel,
        grid=(steps,),
        in_specs=[pl.BlockSpec((COLUMNS // steps, 2, SLOTS, HALF), lambda i: (i, 0, 0, 0))]
        + [whole((WIDTH, FF))] * 4,
        out_specs=[out] * 3,
        out_shape=[jax.ShapeDtypeStruct((RECV, HID), BF16)] * 3,
        compiler_params=pltpu.CompilerParams(vmem_limit_bytes=56 * MIB),
        cost_estimate=pl.CostEstimate(
            flops=4 * RECV * WIDTH * HID, bytes_accessed=14000000, transcendentals=RECV * HID
        ),
        name="forward",
    )(x_recv, gate_a, gate_b, up_a, up_b)


def backward_kernel(
    dy_hbm, hidden_hbm, act_hbm, slope_hbm, gate_a, gate_b, up_a, up_b, down_a, down_b,
    turn_ref, source_ref, lane_ref, out_ref, term_ref,
    dy, hidden, act, slope, ins, down, d_pre, grads, sems,
):
    copies = [
        pltpu.make_async_copy(dy_hbm.at[:, 0], dy.at[:, :, pl.ds(0, HALF)], sems.at[0]),
        pltpu.make_async_copy(dy_hbm.at[:, 1], dy.at[:, :, pl.ds(HALF, HALF)], sems.at[1]),
        pltpu.make_async_copy(down_a, down.at[pl.ds(0, FF)], sems.at[2]),
        pltpu.make_async_copy(down_b, down.at[pl.ds(FF, FF)], sems.at[3]),
        pltpu.make_async_copy(hidden_hbm, hidden, sems.at[4]),
        pltpu.make_async_copy(act_hbm, act, sems.at[5]),
        pltpu.make_async_copy(slope_hbm, slope, sems.at[6]),
    ]
    for i, weight in enumerate((gate_a, up_a, gate_b, up_b)):
        copies.append(
            pltpu.make_async_copy(weight, ins.at[:, pl.ds(i * FF, FF)], sems.at[7 + i])
        )
    for copy in copies:
        copy.start()
    copies[0].wait()
    copies[1].wait()
    copies[2].wait()
    term = jnp.zeros((RECV, 1), F32)
    rows = dy[...].reshape(RECV, WIDTH)
    for i in range(2):
        span = slice(i * FF, (i + 1) * FF)
        if i == 1:
            copies[3].wait()
        d_hidden = lax.dot_general(rows, down[span, :], TURN, preferred_element_type=F32)
        if i == 0:
            copies[4].wait()
            copies[5].wait()
            copies[6].wait()
        term = term + jnp.sum(d_hidden * hidden[:, span].astype(F32), axis=1, keepdims=True)
        first = 2 * i * FF
        d_pre[:, first : first + FF] = (d_hidden * slope[:, span].astype(F32)).astype(BF16)
        d_pre[:, first + FF : first + 2 * FF] = (d_hidden * act[:, span].astype(F32)).astype(BF16)
    spread = jnp.where(lane_ref[...] > 0.0, term, 0.0).astype(BF16)
    term_ref[...] = jnp.dot(source_ref[...], spread, preferred_element_type=F32)
    for copy in copies[7:]:
        copy.wait()
    for q in range(QUARTERS):
        span = slice(q * QWIDTH, (q + 1) * QWIDTH)
        part = lax.dot_general(d_pre[...], ins[span, :], TURN, preferred_element_type=F32)
        grads[:, q] = part.astype(BF16).reshape(COLUMNS, SLOTS, QWIDTH)
    for pair in range(COLUMNS // 2):
        piece = grads[2 * pair : 2 * pair + 2].reshape(2 * QUARTERS * SLOTS, QWIDTH)
        moved = jnp.dot(turn_ref[...], piece, preferred_element_type=F32).astype(BF16)
        out_ref[:, pair * 2 * PIECE : (pair + 1) * 2 * PIECE, :] = moved.reshape(
            Z, 2 * PIECE, QWIDTH
        )


def backward(dy_recv, hidden, act, slope, weights):
    far = pl.BlockSpec(memory_space=pl.ANY)
    near = pl.BlockSpec(memory_space=pltpu.VMEM)
    back_shape = (Z, COLUMNS * PIECE, QWIDTH)
    return pl.pallas_call(
        backward_kernel,
        in_specs=[far] * 10 + [near] * 3,
        out_specs=[near, near],
        out_shape=[
            jax.ShapeDtypeStruct(back_shape, BF16),
            jax.ShapeDtypeStruct((Z, 128), F32),
        ],
        scratch_shapes=[
            pltpu.VMEM((COLUMNS, SLOTS, WIDTH), BF16),
            pltpu.VMEM((RECV, HID), BF16),
            pltpu.VMEM((RECV, HID), BF16),
            pltpu.VMEM((RECV, HID), BF16),
            pltpu.VMEM((WIDTH, 2 * HID), BF16),
            pltpu.VMEM((HID, WIDTH), BF16),
            pltpu.VMEM((RECV, 2 * HID), BF16),
            pltpu.VMEM((COLUMNS, QUARTERS, SLOTS, QWIDTH), BF16),
            pltpu.SemaphoreType.DMA((11,)),
        ],
        compiler_params=pltpu.CompilerParams(vmem_limit_bytes=56 * MIB),
        cost_estimate=pl.CostEstimate(
            flops=6 * RECV * WIDTH * HID, bytes_accessed=20000000, transcendentals=0
        ),
        name="backward",
    )(dy_recv, hidden, act, slope, *weights, turn_rows(), *term_tables())


def place_kernel(half_ref, ids_ref, gates_ref, spread_ref, wanted_ref, place_ref, code_ref):
    lane = lax.broadcasted_iota(jnp.int32, (TOK, EXPERTS), 1)
    core = (lane % 2).astype(F32)
    expert = lane - lane % 2 + half_ref[0]
    member = jnp.zeros((TOK, EXPERTS), F32)
    gate = jnp.zeros((TOK, EXPERTS), F32)
    for k in range(TOPK):
        same = ids_ref[:, k : k + 1] == expert
        value = gates_ref[:, k : k + 1].astype(F32) * (1.0 / 65536.0)
        member = member + jnp.where(same, 1.0, 0.0)
        gate = gate + jnp.where(same, value, 0.0)
    row = lax.broadcasted_iota(jnp.int32, (TOK, TOK), 0)
    column = lax.broadcasted_iota(jnp.int32, (TOK, TOK), 1)
    before = jnp.where(column < row, 1.0, 0.0).astype(BF16)
    rank = jnp.dot(before, member.astype(BF16), preferred_element_type=F32)
    upper = jnp.where(rank >= SHARE, 1.0, 0.0)
    code = jnp.where((member > 0.0) & (upper == core), rank - SHARE * upper, -1.0)
    code_ref[...] = code
    code_wide = jnp.dot(code.astype(BF16), spread_ref[...], preferred_element_type=F32)
    gate_wide = jnp.dot(gate.astype(BF16), spread_ref[...], preferred_element_type=F32)
    for q in range(QUARTERS):
        hit = code_wide == wanted_ref[q : q + 1, :]
        place_ref[q * TOK : (q + 1) * TOK, :] = jnp.where(hit, gate_wide, 0.0).astype(BF16)


def make_place(half, ids, gates):
    return pl.pallas_call(
        place_kernel,
        grid_spec=pltpu.PrefetchScalarGridSpec(
            num_scalar_prefetch=1,
            grid=(1,),
            in_specs=[
                whole((TOK, TOPK)),
                whole((TOK, TOPK)),
                whole((EXPERTS, BACK)),
                whole((8, BACK)),
            ],
            out_specs=[whole((QUARTERS * TOK, BACK)), whole((TOK, EXPERTS))],
        ),
        out_shape=[
            jax.ShapeDtypeStruct((QUARTERS * TOK, BACK), BF16),
            jax.ShapeDtypeStruct((TOK, EXPERTS), F32),
        ],
        compiler_params=pltpu.CompilerParams(vmem_limit_bytes=40 * MIB),
        cost_estimate=pl.CostEstimate(flops=300000000, bytes_accessed=4000000, transcendentals=0),
        name="place",
    )(half, ids, gates, *place_tables())


def terms_kernel(where_ref, code_ref, ids_ref, *refs):
    parts, (swapped_ref, mine_ref, theirs_ref, every, out) = refs[:5], refs[5:]
    half, core = where_ref[2], where_ref[3]

    def keep(distance, block):
        source = lax.rem(where_ref[1] + 2 * Z - distance, Z)
        every[pl.ds(pl.multiple_of(source * COLUMNS, COLUMNS), COLUMNS), :] = block

    keep(0, parts[0][...])
    keep(4, parts[4][...])
    for i in range(1, 4):
        keep(i + 4 * core, parts[i][...])
        keep(i + 4 * (1 - core), swapped_ref[(i - 1) * COLUMNS : i * COLUMNS, :])
    slot = lax.broadcasted_iota(jnp.int32, (8, 128), 0)
    lane = lax.broadcasted_iota(jnp.int32, (8, 128), 1)
    pick = jnp.where((lane == slot + where_ref[0]) & (slot < SHARE), 1.0, 0.0)
    term = lax.dot_general(
        pick.astype(BF16), every[...].astype(BF16), TURN, preferred_element_type=F32
    )
    found = jnp.zeros((TOK, EXPERTS), F32)
    for s in range(SHARE):
        found = found + jnp.where(code_ref[...] == float(s), term[s : s + 1, :], 0.0)
    column = lax.broadcasted_iota(jnp.int32, (TOK, EXPERTS), 1)
    expert = column - column % 2 + half
    total = jnp.zeros((TOK, 128), F32)
    for k in range(TOPK):
        hit = jnp.where(ids_ref[:, k : k + 1] == expert, found, 0.0)
        total = jnp.where(column == k, jnp.sum(hit, axis=1, keepdims=True), total)
    out[...] = total
    rows = TOK // 2
    mine_ref[...] = out[pl.ds(pl.multiple_of(half * rows, rows), rows), :]
    theirs_ref[...] = out[pl.ds(pl.multiple_of((1 - half) * rows, rows), rows), :]


def own_terms(where, parts, code, ids):
    near = pl.BlockSpec(memory_space=pltpu.VMEM)
    return pl.pallas_call(
        terms_kernel,
        in_specs=[pl.BlockSpec(memory_space=pltpu.SMEM)] + [near] * (2 + 6),
        out_specs=[near, near],
        out_shape=[jax.ShapeDtypeStruct((TOK // 2, 128), F32)] * 2,
        scratch_shapes=[pltpu.VMEM((EXPERTS, 128), F32), pltpu.VMEM((TOK, 128), F32)],
        cost_estimate=pl.CostEstimate(flops=1000000, bytes_accessed=300000, transcendentals=0),
        name="terms",
    )(where, code, ids, *parts)


def combine_kernel(
    half_ref, place_hbm, back_hbm, mine_ref, theirs_ref, place, back, total, sems
):
    depth = BACK // STEPS
    copies = []
    for i in range(STEPS):
        span = pl.ds(i * depth, depth)
        copies.append(
            (
                pltpu.make_async_copy(place_hbm.at[:, span], place.at[:, span], sems.at[2 * i]),
                pltpu.make_async_copy(back_hbm.at[span], back.at[span], sems.at[2 * i + 1]),
            )
        )
    for pair in copies:
        for copy in pair:
            copy.start()
    for i, pair in enumerate(copies):
        for copy in pair:
            copy.wait()
        span = slice(i * depth, (i + 1) * depth)
        part = jnp.dot(place[:, span], back[span, :], preferred_element_type=F32)
        total[...] = part if i == 0 else total[...] + part
    rows = TOK // 2
    for q in range(QUARTERS):
        span = slice(q * QWIDTH, (q + 1) * QWIDTH)
        own = pl.multiple_of(q * TOK + half_ref[0] * rows, rows)
        other = pl.multiple_of(q * TOK + (1 - half_ref[0]) * rows, rows)
        theirs_ref[:, span] = total[pl.ds(other, rows), :].astype(BF16)
        mine_ref[:, span] = total[pl.ds(own, rows), :]


STEPS = 4


def combine(half, place, back):
    near = pl.BlockSpec(memory_space=pltpu.VMEM)
    return pl.pallas_call(
        combine_kernel,
        in_specs=[
            pl.BlockSpec(memory_space=pltpu.SMEM),
            pl.BlockSpec(memory_space=pl.ANY),
            pl.BlockSpec(memory_space=pl.ANY),
        ],
        out_specs=[near, near],
        out_shape=[
            jax.ShapeDtypeStruct((TOK // 2, WIDTH), F32),
            jax.ShapeDtypeStruct((TOK // 2, WIDTH), BF16),
        ],
        scratch_shapes=[
            pltpu.VMEM((QUARTERS * TOK, BACK), BF16),
            pltpu.VMEM((BACK, QWIDTH), BF16),
            pltpu.VMEM((QUARTERS * TOK, QWIDTH), F32),
            pltpu.SemaphoreType.DMA((2 * STEPS,)),
        ],
        compiler_params=pltpu.CompilerParams(vmem_limit_bytes=56 * MIB),
        cost_estimate=pl.CostEstimate(
            flops=2 * QUARTERS * TOK * BACK * QWIDTH, bytes_accessed=8000000, transcendentals=0
        ),
        name="combine",
    )(half, place, back)


def finish_kernel(mine_ref, theirs_ref, router_ref, d_mine_ref, d_theirs_ref, grad_ref, d_gate_ref):
    total = mine_ref[...] + theirs_ref[...].astype(F32) + router_ref[...]
    grad_ref[...] = total.astype(BF16)
    d_gate_ref[...] = (d_mine_ref[...] + d_theirs_ref[...])[:, :TOPK]


def finish(mine, theirs, router_back, d_mine, d_theirs):
    near = pl.BlockSpec(memory_space=pltpu.VMEM)
    rows = TOK // 2
    return pl.pallas_call(
        finish_kernel,
        in_specs=[near] * 5,
        out_specs=[near, near],
        out_shape=[
            jax.ShapeDtypeStruct((rows, WIDTH), BF16),
            jax.ShapeDtypeStruct((rows, TOPK), F32),
        ],
        compiler_params=pltpu.CompilerParams(vmem_limit_bytes=16 * MIB),
        cost_estimate=pl.CostEstimate(flops=1000000, bytes_accessed=1500000, transcendentals=0),
        name="finish",
    )(mine, theirs, router_back, d_mine, d_theirs)


def on_device(tokens, grad_out, router_weight, expert_ids, gate_fixed, w_gate, w_up, w_down):
    z = lax.axis_index("z")
    yl = lax.axis_index("yl")
    c = lax.axis_index("c")
    column = (lax.axis_index("yh") * 4 + lax.axis_index("x")) * 2 + c
    at_home = c == yl
    half_index = yl.reshape(1).astype(jnp.int32)

    def cross(block):
        return lax.ppermute(block, ("c", "yl"), [(1, 2), (2, 1)])

    def other_core(block):
        return lax.ppermute(block, "c", [(0, 1), (1, 0)])

    def half_columns(block):
        return lax.dynamic_slice_in_dim(block, yl * HALF, HALF, 1)

    def exchange(block):
        return lax.all_to_all(block, PLANE, split_axis=0, concat_axis=0, tiled=True)

    def ring(block):
        ahead = [(i, (i + 1) % Z) for i in range(Z)]
        behind = [(i, (i - 1) % Z) for i in range(Z)]
        found, left, right = [block], block, block
        for _ in range(3):
            left, right = lax.ppermute(left, "z", ahead), lax.ppermute(right, "z", behind)
            found += [left, right]
        both = [(2 * i, 2 * j) for i, j in ahead] + [(2 * i + 1, 2 * j + 1) for i, j in behind]
        return [*found, lax.ppermute(jnp.where(c == 0, left, right), ("z", "c"), both)]

    plane = z.reshape(1).astype(jnp.int32)
    gate_c, up_c, down_c = cross(w_gate[0]), cross(w_up[0]), cross(w_down[0])
    blank = jnp.zeros((TOK, META - TOPK), BF16)
    x_chunks = ring(
        jnp.concatenate([half_columns(tokens), expert_ids.astype(BF16), blank], axis=1)
    )
    dy_half, x_chunks[6] = lax.optimization_barrier((half_columns(grad_out), x_chunks[6]))
    dy_chunks = ring(dy_half)
    x_send, code, counts = dispatch(plane, x_chunks)
    x_send, gate_c, up_c, down_c = lax.optimization_barrier((x_send, gate_c, up_c, down_c))
    gate_a = jnp.where(at_home, w_gate[0], gate_c)
    up_a = jnp.where(at_home, w_up[0], up_c)
    down_a = jnp.where(at_home, w_down[0], down_c)
    x_recv = exchange(x_send)
    gate_b, up_b, down_b = other_core(gate_a), other_core(up_a), other_core(down_a)
    dy_send = dispatch(plane, dy_chunks, code=code)
    dy_recv = exchange(dy_send)
    hidden, act, slope = forward(
        x_recv.reshape(COLUMNS, 2, SLOTS, HALF), gate_a, gate_b, up_a, up_b
    )
    grads, terms = backward(
        dy_recv.reshape(COLUMNS, 2, SLOTS, HALF),
        hidden,
        act,
        slope,
        (gate_a, gate_b, up_a, up_b, down_a, down_b),
    )
    back = lax.all_to_all(
        grads.reshape(BACK, QWIDTH), SAME_SPLIT, split_axis=0, concat_axis=0, tiled=True
    )
    plane_news = lax.all_gather(
        jnp.concatenate([terms, counts], axis=0), ("yh", "x", "c"), axis=0, tiled=False
    )
    load = plane_news[:, Z].sum(axis=0)

    def terms_for(distance):
        return lax.dynamic_index_in_dim(plane_news, (z + distance) % Z, 1, keepdims=False)

    def turned_terms(step):
        route = []
        for i in range(Z):
            for core in range(2):
                distance = step + 4 * core if step < 4 else 4
                route.append((i * 2 + core, (i + distance) % Z * 2 + core))
        distance = step + 4 * c if step < 4 else 4
        return lax.ppermute(terms_for(distance), ("z", "c"), route)

    found_terms = [terms_for(0)] + [turned_terms(step) for step in range(1, 5)]

    half_rows = TOK // 2
    place, own_code = make_place(half_index, expert_ids, gate_fixed)
    swap = [(0, 1), (1, 0)]

    own_tokens = lax.dynamic_slice_in_dim(tokens, yl * half_rows, half_rows, 0)
    logits = jnp.dot(own_tokens, router_weight, preferred_element_type=F32)
    probs = jax.nn.softmax(logits, axis=1)
    share = load * EXPERTS / (EXPERTS * TOK * TOPK)
    d_logits = EXPERTS * probs * (
        share[None, :] - jnp.sum(probs * share[None, :], axis=1, keepdims=True)
    )
    router_back = lax.dot_general(
        d_logits.astype(BF16), router_weight, TURN, preferred_element_type=F32
    )

    back, router_back, place, found_terms = lax.optimization_barrier(
        (back, router_back, place, found_terms)
    )
    swapped = other_core(jnp.concatenate(found_terms[1:4], axis=0))
    mine, theirs = combine(half_index, place, back)
    theirs, swapped = lax.optimization_barrier((theirs, swapped))
    theirs = lax.ppermute(theirs, "yl", swap)
    where = jnp.stack([column * SHARE, z, yl, c]).astype(jnp.int32)
    d_mine, d_theirs = own_terms(where, [*found_terms, swapped], own_code, expert_ids)
    d_theirs = lax.ppermute(d_theirs, "yl", swap)
    grad_tokens, d_gate = finish(mine, theirs, router_back, d_mine, d_theirs)
    return grad_tokens, d_gate, d_logits


def solution(mesh):
    fine = Mesh(mesh.devices.reshape(8, 2, 4, 2, 2), ("z", "yh", "x", "c", "yl"))
    return jax.shard_map(
        on_device,
        mesh=fine,
        in_specs=(
            P(SAME_SPLIT, None),
            P(SAME_SPLIT, None),
            P(),
            P(SAME_SPLIT, None),
            P(SAME_SPLIT, None),
            P(SAME_SPLIT, None, "yl"),
            P(SAME_SPLIT, None, "yl"),
            P(SAME_SPLIT, "yl", None),
        ),
        out_specs=(
            P(SAME_SPLIT + ("yl",), None),
            P(SAME_SPLIT + ("yl",), None),
            P(SAME_SPLIT + ("yl",), None),
        ),
        check_vma=False,
    )
```
